32 devices in a mesh: groups: 2 (over y), dp: 4 (over z), owner: 2 (over x), seq: 2 (over core).
Axes of the slice: x: 2, y: 2, z: 4, core: 2. Of those that a mesh axis runs over, the one named last changes fastest.
Arguments:
- tokens: bfloat16 [4096, 6144], P(('groups', 'dp', 'seq')), parts along dimension 0, may hold values from -16 to 16
- document_lengths: int32 [8, 4], P(('groups', 'dp')), parts along dimension 0, may hold values from 1 to 384, 512 in all within a row
- document_adapter: int32 [8, 4], P(('groups', 'dp')), parts along dimension 0, may hold values from 0 to 3
- adapter_stored_row: int32 [4], replicated, may hold values from 0 to 3, each once
- query_weight: bfloat16 [6144, 3072], P('dp', 'owner'), may hold values from -0.078125 to 0.078125
- key_weight: bfloat16 [6144, 512], P('dp', 'owner'), may hold values from -0.078125 to 0.078125
- value_weight: bfloat16 [6144, 512], P('dp', 'owner'), may hold values from -0.078125 to 0.078125
- adapter_down_weight: bfloat16 [4, 6144, 8], P('dp', 'owner'), may hold values from -0.078125 to 0.078125
- adapter_up_weight: bfloat16 [4, 8, 3072], P('dp', None, 'owner'), may hold values from -2 to 2
- output_cotangent: bfloat16 [4096, 3072], P(('groups', 'dp', 'seq'), 'owner'), parts along dimension 0, may hold values from -6 to 6
Outputs:
- attended: bfloat16 [4096, 3072], P(('groups', 'dp', 'seq'), 'owner'), parts along dimension 0
- grad_down: float32 [8, 6144, 8], P(('groups', 'dp'), ('owner', 'seq')), parts along dimension 0
- grad_up: float32 [8, 8, 3072], P(('groups', 'dp'), None, ('owner', 'seq')), parts along dimension 0
The draws below stay inside these ranges and needn't reach their ends.
There are 2 independent parts, one for each index of `groups`. The reference program is written for one: setup_inputs(seed, part) draws one part's arguments, and reference() takes and returns one part's arrays. A program takes and returns all parts, laid end to end along the dimension named above; an argument that names none is the same for every part. Nothing has to cross between parts.
Inputs may be any that keep to these rules, and one draw needn't show every extreme that they name: `document_lengths`: the 4 lengths of one sequence sum to 512. `adapter_stored_row`: each of the 4 stored rows once.
All inputs are finite; a program needn't handle non-finite values.
Results may differ from the reference program's by a relative error of at most 0.0085.
The reference program's roundings to bfloat16 on the way count: a program that leaves them out, or rounds other values in their place, can miss the bound.
Values may be sent and summed in bfloat16 or wider, within the bound.
A program may use at most 128 MiB of HBM per device.

```python
import math
import jax
import jax.numpy as jnp
import numpy as np
from jax import lax

MODEL_WIDTH = 6144
QUERY_HEADS = 24
KEY_VALUE_HEADS = 4
HEAD_SIZE = 128
ADAPTER_RANK = 8
DOCS = 4
TOK_DEV = 256
SEQUENCE_LENGTH = 512
TOKEN_COUNT = 2048
ADAPTER_COUNT = 4
N_DP = 4
N_SEQ = 2


def draw_tokens(key, part):
    key = jax.random.fold_in(key, 11)
    normal_key = jax.random.fold_in(key, 0)
    normals = jax.random.normal(normal_key, (TOKEN_COUNT, MODEL_WIDTH), jnp.float32)
    normals = jnp.clip(normals, -6.0, 6.0)
    return normals.astype(jnp.bfloat16)


def set_ends(array, key, smallest, largest):
    longest = array.shape.index(max(array.shape))
    spots = []
    for shift in (0, 1):
        where = [jax.random.randint(jax.random.fold_in(key, axis), (), 0, length) for axis, length in enumerate(array.shape)]
        where[longest] = (where[longest] + shift) % array.shape[longest]
        spots.append(tuple(where))
    return array.at[spots[0]].set(smallest).at[spots[1]].set(largest)


def steps_of(stream_key, dims, cuts, smallest, largest):
    def one(axis_at, parts):
        draws = jax.random.uniform(jax.random.fold_in(jax.random.fold_in(stream_key, 6), axis_at), (parts,), jnp.float32, smallest / len(cuts), largest / len(cuts))
        return jnp.repeat(jnp.exp(draws), dims[axis_at] // parts).reshape((-1,) + (1,) * (len(dims) - axis_at - 1))

    gain = one(*cuts[0])
    for cut in cuts[1:]:
        gain = gain * one(*cut)
    return gain


def split_up(amount, total, bound, lean):
    portions = [(1 << 20) // math.isqrt(rank ** lean) + 1 for rank in range(2, amount + 1)]
    surplus, counts = total - bound - (amount - 1), [1] * (amount - 1)
    while surplus > 0:
        candidates = [i for i in range(amount - 1) if counts[i] < bound]
        mass, left = sum([portions[i] for i in candidates]), surplus
        for i in candidates:
            extra = min(bound - counts[i], max(1, left * portions[i] // mass), surplus)
            counts[i] = counts[i] + extra
            surplus = surplus - extra
    return np.array([bound] + counts)


def uneven(own_key, amount, total, reach, slope):
    if amount == 2:
        one = jax.random.randint(own_key, (), max(1, total - reach), min(reach, total - 1) + 1)
        return jnp.stack([one, total - one])
    tallies = jnp.asarray(split_up(amount, total, reach, slope), jnp.int32)
    couples = (amount - 1) // 2
    source_of, sink = tallies[1:1 + 2 * couples:2], tallies[2:2 + 2 * couples:2]
    room = jnp.minimum(source_of - 1, reach - sink)
    passed = jax.random.randint(jax.random.fold_in(own_key, 1), (couples,), 0, 1 << 20) % (room + 1)
    tallies = tallies.at[1:1 + 2 * couples:2].set(source_of - passed).at[2:2 + 2 * couples:2].set(sink + passed)
    return tallies[jax.random.permutation(jax.random.fold_in(own_key, 2), amount)]


def centred(own_key, shape, scale, limit, cuts=(), dtype=jnp.bfloat16):
    factor_of = steps_of(own_key, shape, cuts, -0.22, 0.18) if cuts else 1.0
    entries = jax.random.normal(own_key, shape, jnp.float32) * scale * factor_of
    return jnp.minimum(jnp.maximum(entries, -limit), limit).astype(dtype)


def setup_inputs(seed: int = 0, part: int = 0) -> dict:
    seeds = jax.random.split(jax.random.key(seed), 11)
    own_keys = jax.random.split(jax.random.fold_in(seeds[10], part), 11)
    return {
        "tokens": draw_tokens(jax.random.fold_in(jax.random.fold_in(seeds[10], part), 71), part),
        "document_lengths": jax.vmap(lambda own: uneven(own, DOCS, TOK_DEV * N_SEQ, TOK_DEV * N_SEQ * 3 // 4, 0))(jax.random.split(own_keys[1], N_DP)).reshape((N_DP, DOCS)).astype(jnp.int32),
        "document_adapter": set_ends(jax.random.randint(own_keys[2], (N_DP, DOCS), 0, ADAPTER_COUNT), jax.random.fold_in(own_keys[2], 1), 0, ADAPTER_COUNT - 1).astype(jnp.int32),
        "adapter_stored_row": jax.random.permutation(seeds[3], ADAPTER_COUNT).astype(jnp.int32),
        "query_weight": centred(seeds[4], (MODEL_WIDTH, QUERY_HEADS * HEAD_SIZE), MODEL_WIDTH ** -0.5, 0.078125, ((0, 4), (1, 2))),
        "key_weight": centred(seeds[5], (MODEL_WIDTH, KEY_VALUE_HEADS * HEAD_SIZE), MODEL_WIDTH ** -0.5, 0.078125, ((0, 4), (1, 2))),
        "value_weight": centred(seeds[6], (MODEL_WIDTH, KEY_VALUE_HEADS * HEAD_SIZE), MODEL_WIDTH ** -0.5, 0.078125, ((0, 4), (1, 2))),
        "adapter_down_weight": centred(seeds[7], (ADAPTER_COUNT, MODEL_WIDTH, ADAPTER_RANK), MODEL_WIDTH ** -0.5, 0.078125, ((0, 4), (1, 2))),
        "adapter_up_weight": centred(seeds[8], (ADAPTER_COUNT, ADAPTER_RANK, QUERY_HEADS * HEAD_SIZE), ADAPTER_RANK ** -0.5, 2.0, ((0, 4), (2, 2))),
        "output_cotangent": centred(own_keys[9], (TOKEN_COUNT, QUERY_HEADS * HEAD_SIZE), 1.0, 6.0, ((0, 8), (1, 2))),
    }


rope_base = 1000000.0
neg_big = -1e+30

def rotary_apply(rotated_in, token_positions, direction):
    half_width = rotated_in.shape[-1] // 2
    frequency = rope_base ** (-(jnp.arange(half_width).astype(jnp.float32) * 2.0 / rotated_in.shape[-1]))
    angles = token_positions.astype(jnp.float32)[:, None] * frequency[None, :]
    cosines = jnp.cos(angles)[:, None, :]
    sines = direction * jnp.sin(angles)[:, None, :]
    front_half = rotated_in[..., :half_width]
    back_half = rotated_in[..., half_width:]
    return jnp.concatenate([front_half * cosines - back_half * sines, back_half * cosines + front_half * sines], axis=-1)

def reference(tokens, document_lengths, document_adapter, adapter_stored_row, query_weight, key_weight, value_weight, adapter_down_weight, adapter_up_weight, output_cotangent):
    doc_ends = jnp.cumsum(document_lengths, axis=1)
    where_at = jnp.arange(SEQUENCE_LENGTH).astype(jnp.int32)
    document_of_token = lax.optimization_barrier(jnp.sum((where_at[None, :, None] >= doc_ends[:, None, :]).astype(jnp.int32), axis=2))
    in_document = document_of_token[:, :, None] == jnp.arange(DOCS).astype(jnp.int32)[None, None, :]
    adapter_of = lax.optimization_barrier(jnp.sum(jnp.where(in_document, document_adapter[:, None, :], 0), axis=2)).reshape(TOKEN_COUNT)
    adapter_ids = jnp.arange(ADAPTER_COUNT).astype(jnp.int32)
    stored_row = lax.optimization_barrier(jnp.sum(jnp.where(adapter_of[:, None] == adapter_ids[None, :], adapter_stored_row[None, :], 0), axis=1))
    chooser = (stored_row[:, None] == adapter_ids[None, :]).astype(jnp.float32)
    down_weight_flat = jnp.transpose(adapter_down_weight, (1, 0, 2)).reshape(MODEL_WIDTH, ADAPTER_COUNT * ADAPTER_RANK)
    up_weight_flat = adapter_up_weight.reshape(ADAPTER_COUNT * ADAPTER_RANK, QUERY_HEADS * HEAD_SIZE)
    every_low = jnp.dot(tokens, down_weight_flat, preferred_element_type=jnp.float32).reshape(TOKEN_COUNT, ADAPTER_COUNT, ADAPTER_RANK)
    low_rank = lax.optimization_barrier(jnp.sum(every_low * chooser[:, :, None], axis=1)).astype(jnp.bfloat16)
    spread = (low_rank.astype(jnp.float32)[:, None, :] * chooser[:, :, None]).astype(jnp.bfloat16).reshape(TOKEN_COUNT, ADAPTER_COUNT * ADAPTER_RANK)
    query_raw = jnp.dot(tokens, query_weight, preferred_element_type=jnp.float32) + jnp.dot(spread, up_weight_flat, preferred_element_type=jnp.float32)
    token_positions = jnp.tile(where_at, N_DP)
    query_rows = rotary_apply(query_raw.reshape(TOKEN_COUNT, QUERY_HEADS, HEAD_SIZE), token_positions, 1.0).astype(jnp.bfloat16)
    key_rows = rotary_apply(jnp.dot(tokens, key_weight, preferred_element_type=jnp.float32).reshape(TOKEN_COUNT, KEY_VALUE_HEADS, HEAD_SIZE), token_positions, 1.0).astype(jnp.bfloat16)
    value_rows = jnp.dot(tokens, value_weight, preferred_element_type=jnp.float32).astype(jnp.bfloat16).reshape(TOKEN_COUNT, KEY_VALUE_HEADS, HEAD_SIZE)
    head_grouping = QUERY_HEADS // KEY_VALUE_HEADS
    score_scale = 1.0 / math.sqrt(HEAD_SIZE)

    def one_sequence(sequence_entries):
        query_input, keys_in, values_in, output_gradient, doc_ids = sequence_entries
        query_input = query_input.reshape(SEQUENCE_LENGTH, KEY_VALUE_HEADS, head_grouping, HEAD_SIZE).astype(jnp.float32)
        keys_in = keys_in.astype(jnp.float32)
        values_in = values_in.astype(jnp.float32)
        output_gradient = output_gradient.reshape(SEQUENCE_LENGTH, KEY_VALUE_HEADS, head_grouping, HEAD_SIZE).astype(jnp.float32)
        scores = jnp.einsum('qcgd,kcd->cgqk', query_input, keys_in) * score_scale
        allowed = (doc_ids[:, None] == doc_ids[None, :]) & (where_at[:, None] >= where_at[None, :])
        scores = jnp.where(allowed[None, None], scores, neg_big)
        row_max = lax.optimization_barrier(jnp.max(scores, axis=-1, keepdims=True))
        raised = jnp.exp(scores - row_max)
        probability = raised / lax.optimization_barrier(jnp.sum(raised, axis=-1, keepdims=True))
        weights = lax.optimization_barrier(probability.astype(jnp.bfloat16)).astype(jnp.float32)
        attended_seq = jnp.einsum('cgqk,kcd->qcgd', weights, values_in).astype(jnp.bfloat16)
        dprob = jnp.einsum('qcgd,kcd->cgqk', output_gradient, values_in)
        row_delta = lax.optimization_barrier(jnp.sum(probability * dprob, axis=-1, keepdims=True))
        dscore = lax.optimization_barrier((probability * (dprob - row_delta)).astype(jnp.bfloat16)).astype(jnp.float32)
        grad_rot = jnp.einsum('cgqk,kcd->qcgd', dscore, keys_in) * score_scale
        return (attended_seq.reshape(SEQUENCE_LENGTH, QUERY_HEADS * HEAD_SIZE), grad_rot.reshape(SEQUENCE_LENGTH, QUERY_HEADS, HEAD_SIZE))
    sequence_entries = (query_rows.reshape(N_DP, SEQUENCE_LENGTH, QUERY_HEADS * HEAD_SIZE), key_rows.reshape(N_DP, SEQUENCE_LENGTH, KEY_VALUE_HEADS, HEAD_SIZE), value_rows.reshape(N_DP, SEQUENCE_LENGTH, KEY_VALUE_HEADS, HEAD_SIZE), output_cotangent.reshape(N_DP, SEQUENCE_LENGTH, QUERY_HEADS * HEAD_SIZE), document_of_token)
    attended, grad_rot = lax.map(one_sequence, sequence_entries)
    attended = attended.reshape(TOKEN_COUNT, QUERY_HEADS * HEAD_SIZE)
    grad_query = rotary_apply(grad_rot.reshape(TOKEN_COUNT, QUERY_HEADS, HEAD_SIZE), token_positions, -1.0).astype(jnp.bfloat16).reshape(TOKEN_COUNT, QUERY_HEADS * HEAD_SIZE)
    every_mid = jnp.dot(grad_query, up_weight_flat.T, preferred_element_type=jnp.float32).reshape(TOKEN_COUNT, ADAPTER_COUNT, ADAPTER_RANK)
    mid_rank = lax.optimization_barrier(jnp.sum(every_mid * chooser[:, :, None], axis=1)).astype(jnp.bfloat16)
    spread_mid = (mid_rank.astype(jnp.float32)[:, None, :] * chooser[:, :, None]).astype(jnp.bfloat16).reshape(TOKEN_COUNT, ADAPTER_COUNT * ADAPTER_RANK)
    grad_down = jnp.dot(tokens.T, spread_mid, preferred_element_type=jnp.float32).reshape(MODEL_WIDTH, ADAPTER_COUNT, ADAPTER_RANK)
    grad_down = jnp.transpose(grad_down, (1, 0, 2))
    grad_up = jnp.dot(spread.T, grad_query, preferred_element_type=jnp.float32).reshape(ADAPTER_COUNT, ADAPTER_RANK, QUERY_HEADS * HEAD_SIZE)
    return (attended, grad_down, grad_up)
```

```python
import functools
import math

import jax
import jax.numpy as jnp
from jax import lax
from jax.experimental import pallas as pl
from jax.experimental.pallas import tpu as pltpu
from jax.sharding import PartitionSpec as P

MESH = pl.DeviceIdType.MESH

HEAD_SIZE = 128


rope_base = 1000000.0
neg_big = -1e30


def rotary_apply(rotated_in, token_positions, direction):
    half_width = rotated_in.shape[-1] // 2
    frequency = rope_base ** (
        -(jnp.arange(half_width).astype(jnp.float32) * 2.0 / rotated_in.shape[-1])
    )
    angles = token_positions.astype(jnp.float32)[:, None] * frequency[None, :]
    cosines = jnp.cos(angles)[:, None, :]
    sines = direction * jnp.sin(angles)[:, None, :]
    front_half = rotated_in[..., :half_width]
    back_half = rotated_in[..., half_width:]
    return jnp.concatenate(
        [front_half * cosines - back_half * sines, back_half * cosines + front_half * sines],
        axis=-1,
    )


def doc_number(token_positions, doc_ends):
    return jnp.sum((token_positions[:, None] >= doc_ends[None, :]).astype(jnp.int32), axis=1)


def project_kernel(
    n, chunks, presplit,
    x_ref, wq_ref, wk_ref, wv_ref, out_ref,
    held, xs, load_sem, x_sem,
    up_send, down_send, y_send, core_send, z_recv, y_recv, core_recv,
):
    depth = wq_ref.shape[0]
    piece = depth // 4
    rows = piece // chunks
    g = lax.axis_index("groups")
    z = lax.axis_index("dp")
    s = lax.axis_index("seq")
    above = n - 1 - z
    below = z
    both = jnp.minimum(above, below)

    copies = []
    at = 0
    for i, ref in enumerate((wq_ref, wk_ref, wv_ref)):
        width = ref.shape[1]
        copies.append(
            pltpu.make_async_copy(ref, held.at[z, :, pl.ds(at, width)], load_sem.at[i])
        )
        at += width
    x_copies = []
    for d in range(n):
        src = x_ref.at[d] if presplit else x_ref.at[:, pl.ds(d * depth, depth)]
        x_copies.append(pltpu.make_async_copy(src, xs.at[d], x_sem.at[d]))
    for c in copies + x_copies:
        c.start()

    barrier = pltpu.get_barrier_semaphore()
    pl.semaphore_signal(barrier, inc=1, device_id={"groups": 1 - g}, device_id_type=MESH)
    pl.semaphore_signal(barrier, inc=1, device_id={"seq": 1 - s}, device_id_type=MESH)

    @pl.when(z > 0)
    def _():
        pl.semaphore_signal(barrier, inc=1, device_id={"dp": z - 1}, device_id_type=MESH)

    @pl.when(z < n - 1)
    def _():
        pl.semaphore_signal(barrier, inc=1, device_id={"dp": z + 1}, device_id_type=MESH)

    pl.semaphore_wait(barrier, 2 + jnp.where(z > 0, 1, 0) + jnp.where(z < n - 1, 1, 0))

    for c in copies:
        c.wait()

    def part(d, gg, ss, c):
        start = pl.multiple_of(((gg * 2 + ss) * chunks + c) * rows, 16)
        return held.at[d, pl.ds(start, rows), :]

    def move(d, gg, ss, c, send, recv, target):
        ref = part(d, gg, ss, c)
        return pltpu.make_async_remote_copy(
            src_ref=ref, dst_ref=ref, send_sem=send, recv_sem=recv,
            device_id=target, device_id_type=MESH,
        )

    def to_below(d, c):
        return move(d, g, s, c, down_send.at[d, c], z_recv.at[d, c], {"dp": jnp.maximum(z - 1, 0)})

    def to_above(d, c):
        return move(d, g, s, c, up_send.at[d, c], z_recv.at[d, c], {"dp": jnp.minimum(z + 1, n - 1)})

    def to_group(d, c):
        return move(d, g, s, c, y_send.at[d, c], y_recv.at[d, c], {"groups": 1 - g})

    def from_group(d, c):
        return move(d, 1 - g, s, c, y_send.at[d, c], y_recv.at[d, c], {"groups": 1 - g})

    def to_core(d, gg, c, k):
        return move(d, gg, s, c, core_send.at[d, c, k], core_recv.at[d, c, k], {"seq": 1 - s})

    def from_core(d, gg, c, k):
        return move(d, gg, 1 - s, c, core_send.at[d, c, k], core_recv.at[d, c, k], {"seq": 1 - s})

    def send_own(c):
        @pl.when(z > 0)
        def _():
            to_below(z, c).start()

        @pl.when(z < n - 1)
        def _():
            to_above(z, c).start()

    ahead = min(2, chunks)
    for c in range(ahead):
        send_own(c)
    for c in x_copies:
        c.wait()

    tile = 512
    tiles = out_ref.shape[1] // tile

    def multiply(d, first):
        def body(j, _):
            cols = pl.ds(pl.multiple_of(j * tile, tile), tile)
            term = jnp.dot(xs[d], held[d, :, cols], preferred_element_type=jnp.float32)
            if first:
                out_ref[:, cols] = term
            else:
                out_ref[:, cols] += term
            return 0

        lax.fori_loop(0, tiles, body, 0)

    multiply(z, True)

    def shard_of(k):
        paired = k < 2 * both
        half = k // 2
        single = jnp.where(above > below, z + 1 + (k - both), z - 1 - (k - both))
        return jnp.where(paired, jnp.where(k % 2 == 0, z + 1 + half, z - 1 - half), single)

    def event(i):
        paired = i < 2 * both * chunks
        t = i // 2
        t2 = i - both * chunks
        up = jnp.where(paired, i % 2 == 0, above > below)
        t = jnp.where(paired, t, t2)
        return jnp.where(up, z + 1 + t // chunks, z - 1 - t // chunks), t % chunks

    def land(d, c, onward, more):
        to_below(d, c).wait_recv()

        @pl.when(more)
        def _():
            onward(d, c).start()

        to_group(d, c).start()
        to_core(d, g, c, 0).start()

    lag = min(2, chunks - 1)

    def step(t, _):
        @pl.when(t + ahead < chunks)
        def _():
            send_own(jnp.minimum(t + ahead, chunks - 1))

        @pl.when(t < above * chunks)
        def _():
            land(jnp.minimum(z + 1 + t // chunks, n - 1), t % chunks, to_below, z > 0)

        @pl.when(t < below * chunks)
        def _():
            land(jnp.maximum(z - 1 - t // chunks, 0), t % chunks, to_above, z < n - 1)

        @pl.when(t >= lag)
        def _():
            cross(t - lag)

        return 0

    def cross(i):
        d, c = event(i)
        from_group(d, c).wait_recv()
        to_core(d, 1 - g, c, 1).start()

    def finish(k):
        d = shard_of(k)

        def body(c, _):
            from_core(d, g, c, 0).wait_recv()
            from_core(d, 1 - g, c, 1).wait_recv()
            return 0

        lax.fori_loop(0, chunks, body, 0)
        multiply(d, False)

    def phase(p, _):
        lax.fori_loop(p * chunks, (p + 1) * chunks, step, 0)

        @pl.when(p >= 2)
        def _():
            finish(jnp.maximum(p - 2, 0))

        return 0

    total = (n - 1) * chunks
    lax.fori_loop(0, n - 1, phase, 0)
    lax.fori_loop(total - lag, total, lambda i, _: (cross(i), 0)[1], 0)
    for k in range(max(n - 3, 0), n - 1):
        finish(jnp.int32(k))

    def drain(i, _):
        d = i // chunks
        c = i % chunks
        mine = d == z

        @pl.when(jnp.logical_and(d >= z, z > 0))
        def _():
            to_below(d, c).wait_send()

        @pl.when(jnp.logical_and(d <= z, z < n - 1))
        def _():
            to_above(d, c).wait_send()

        @pl.when(jnp.logical_not(mine))
        def _():
            to_group(d, c).wait_send()
            to_core(d, g, c, 0).wait_send()
            to_core(d, 1 - g, c, 1).wait_send()

        return 0

    lax.fori_loop(0, n * chunks, drain, 0)


def project(tokens, query_weight, key_weight, value_weight):
    n = lax.axis_size("dp")
    row_count = tokens.shape[0]
    depth = query_weight.shape[0]
    cols = query_weight.shape[1] + key_weight.shape[1] + value_weight.shape[1]
    piece = depth // 4
    chunks = max(c for c in range(1, 9) if piece % c == 0 and (piece // c) % 16 == 0)
    presplit = depth % 128 != 0
    if presplit:
        tokens = jnp.transpose(tokens.reshape(row_count, n, depth), (1, 0, 2))
    dma = pltpu.SemaphoreType.DMA
    return pl.pallas_call(
        functools.partial(project_kernel, n, chunks, presplit),
        out_shape=jax.ShapeDtypeStruct((row_count, cols), jnp.float32),
        in_specs=[pl.BlockSpec(memory_space=pl.ANY)] * 4,
        out_specs=pl.BlockSpec(memory_space=pltpu.VMEM),
        scratch_shapes=[
            pltpu.VMEM((n, depth, cols), jnp.bfloat16),
            pltpu.VMEM((n, row_count, depth), jnp.bfloat16),
            dma((3,)),
            dma((n,)),
            dma((n, chunks)),
            dma((n, chunks)),
            dma((n, chunks)),
            dma((n, chunks, 2)),
            dma((n, chunks)),
            dma((n, chunks)),
            dma((n, chunks, 2)),
        ],
        compiler_params=pltpu.CompilerParams(
            collective_id=0, has_side_effects=True, vmem_limit_bytes=50 * 2**20
        ),
        cost_estimate=pl.CostEstimate(
            flops=2 * row_count * n * depth * cols,
            bytes_accessed=2 * n * depth * cols,
            transcendentals=0,
        ),
    )(tokens, query_weight, key_weight, value_weight)


def shards(
    tokens,
    document_lengths,
    document_adapter,
    adapter_stored_row,
    query_weight,
    key_weight,
    value_weight,
    adapter_down_weight,
    adapter_up_weight,
    output_cotangent,
):
    row_count = tokens.shape[0]
    quarter_part = adapter_down_weight.shape[1]
    adapter_rank_size = adapter_down_weight.shape[2]
    query_cols = query_weight.shape[1]
    key_cols = key_weight.shape[1]
    head_count = query_cols // HEAD_SIZE
    key_heads = key_cols // HEAD_SIZE
    head_grouping = head_count // key_heads
    doc_count = document_lengths.shape[1]
    seq_devices = lax.axis_size("seq")
    adapters = lax.axis_size("dp")
    seq_at = lax.axis_index("seq")
    owner_at = lax.axis_index("owner")
    score_scale = 1.0 / math.sqrt(HEAD_SIZE)
    doc_ends = jnp.cumsum(document_lengths[0])
    own_positions = seq_at * row_count + jnp.arange(row_count, dtype=jnp.int32)
    doc_mine = doc_number(own_positions, doc_ends)
    in_document = doc_mine[:, None] == jnp.arange(doc_count, dtype=jnp.int32)[None, :]
    adapter_of = jnp.sum(jnp.where(in_document, document_adapter[0][None, :], 0), axis=1)
    adapter_ids = jnp.arange(adapters, dtype=jnp.int32)
    stored_row = jnp.sum(
        jnp.where(adapter_of[:, None] == adapter_ids[None, :], adapter_stored_row[None, :], 0),
        axis=1,
    )
    chooser = (stored_row[:, None] == adapter_ids[None, :]).astype(jnp.float32)
    projected = project(tokens, query_weight, key_weight, value_weight)
    base_query = projected[:, :query_cols]
    base_key = projected[:, query_cols : query_cols + key_cols]
    base_value = projected[:, query_cols + key_cols :]
    down_rows = lax.all_gather(jnp.transpose(adapter_down_weight[0]), ("dp", "owner"))
    down_rows = jnp.transpose(
        down_rows.reshape(adapters, -1, adapter_rank_size, quarter_part), (0, 2, 1, 3)
    ).reshape(adapters * adapter_rank_size, tokens.shape[1])
    stored = (None, lax.all_gather(adapter_up_weight, "dp", axis=0, tiled=True))
    up_weight_flat = stored[1].reshape(adapters * adapter_rank_size, query_cols)
    token_quarter = lax.dynamic_slice_in_dim(tokens, owner_at * quarter_part, quarter_part, 1)
    every_low = lax.dot_general(
        tokens, down_rows, (((1,), (1,)), ((), ())), preferred_element_type=jnp.float32
    ).reshape(row_count, adapters, adapter_rank_size)
    low_rank = jnp.sum(every_low * chooser[:, :, None], axis=1).astype(jnp.bfloat16)
    spread = (
        (low_rank.astype(jnp.float32)[:, None, :] * chooser[:, :, None])
        .astype(jnp.bfloat16)
        .reshape(row_count, adapters * adapter_rank_size)
    )
    query_raw = base_query + jnp.dot(spread, up_weight_flat, preferred_element_type=jnp.float32)
    query_rows = rotary_apply(
        query_raw.reshape(row_count, head_count, HEAD_SIZE), own_positions, 1.0
    ).astype(jnp.bfloat16)
    key_rows = rotary_apply(
        base_key.reshape(row_count, key_heads, HEAD_SIZE), own_positions, 1.0
    ).astype(jnp.bfloat16)
    value_rows = base_value.astype(jnp.bfloat16).reshape(row_count, key_heads, HEAD_SIZE)
    key_value = (
        lax.all_gather(key_rows, "seq", axis=0, tiled=True),
        lax.all_gather(value_rows, "seq", axis=0, tiled=True),
    )
    keys_seen = key_value[0]
    values_seen = key_value[1]
    key_positions = jnp.arange(row_count * seq_devices, dtype=jnp.int32)
    key_docs = doc_number(key_positions, doc_ends)
    allowed = (
        (key_docs[None, :] == doc_mine[:, None])
        & (key_positions[None, :] <= own_positions[:, None])
        & (key_positions[None, :] >= 0)
    )
    query_groups = query_rows.reshape(row_count, key_heads, head_grouping, HEAD_SIZE)
    output_gradient = output_cotangent.reshape(row_count, key_heads, head_grouping, HEAD_SIZE)
    scores = (
        jnp.einsum("qcgd,kcd->cgqk", query_groups, keys_seen, preferred_element_type=jnp.float32)
        * score_scale
    )
    scores = jnp.where(allowed[None, None], scores, neg_big)
    row_max = jnp.max(scores, axis=-1, keepdims=True)
    raised = jnp.exp(scores - row_max)
    probability = raised / jnp.sum(raised, axis=-1, keepdims=True)
    weights = probability.astype(jnp.bfloat16)
    attended = jnp.einsum(
        "cgqk,kcd->qcgd", weights, values_seen, preferred_element_type=jnp.float32
    )
    attended = attended.astype(jnp.bfloat16).reshape(row_count, query_cols)
    dprob = jnp.einsum(
        "qcgd,kcd->cgqk", output_gradient, values_seen, preferred_element_type=jnp.float32
    )
    row_delta = jnp.sum(probability * dprob, axis=-1, keepdims=True)
    dscore = (probability * (dprob - row_delta)).astype(jnp.bfloat16)
    grad_rot = (
        jnp.einsum("cgqk,kcd->qcgd", dscore, keys_seen, preferred_element_type=jnp.float32)
        * score_scale
    )
    grad_query = rotary_apply(
        grad_rot.reshape(row_count, head_count, HEAD_SIZE), own_positions, -1.0
    ).astype(jnp.bfloat16)
    grad_query = grad_query.reshape(row_count, query_cols)
    every_mid = lax.dot_general(
        grad_query, up_weight_flat, (((1,), (1,)), ((), ())), preferred_element_type=jnp.float32
    )
    partial_mid = jnp.sum(
        every_mid.reshape(row_count, adapters, adapter_rank_size) * chooser[:, :, None], axis=1
    )
    mid_rank = lax.psum(partial_mid, "owner").astype(jnp.bfloat16)
    spread_mid = (
        (mid_rank.astype(jnp.float32)[:, None, :] * chooser[:, :, None])
        .astype(jnp.bfloat16)
        .reshape(row_count, adapters * adapter_rank_size)
    )
    down_term = lax.dot_general(
        token_quarter, spread_mid, (((0,), (0,)), ((), ())), preferred_element_type=jnp.float32
    )
    down_term = jnp.transpose(
        down_term.reshape(quarter_part, adapters, adapter_rank_size), (1, 0, 2)
    )
    up_term = lax.dot_general(
        spread, grad_query, (((0,), (0,)), ((), ())), preferred_element_type=jnp.float32
    )
    up_term = up_term.reshape(adapters, adapter_rank_size, query_cols)
    down_term = down_term.reshape(
        adapters * seq_devices, quarter_part // seq_devices, adapter_rank_size
    )
    up_term = up_term.reshape(adapters, adapter_rank_size, seq_devices, query_cols // seq_devices)
    up_term = jnp.transpose(up_term, (0, 2, 1, 3)).reshape(
        adapters * seq_devices, adapter_rank_size, query_cols // seq_devices
    )
    gradients = (
        lax.psum_scatter(down_term, ("dp", "seq"), scatter_dimension=0, tiled=True),
        lax.psum_scatter(up_term, ("dp", "seq"), scatter_dimension=0, tiled=True),
    )
    return (attended, gradients[0], gradients[1])


def solution(mesh):
    in_specs = (
        P(("groups", "dp", "seq"), None),
        P(("groups", "dp"), None),
        P(("groups", "dp"), None),
        P(),
        P("dp", "owner"),
        P("dp", "owner"),
        P("dp", "owner"),
        P("dp", "owner", None),
        P("dp", None, "owner"),
        P(("groups", "dp", "seq"), "owner"),
    )
    out_specs = (
        P(("groups", "dp", "seq"), "owner"),
        P(("groups", "dp"), ("owner", "seq"), None),
        P(("groups", "dp"), None, ("owner", "seq")),
    )
    return jax.shard_map(shards, mesh=mesh, in_specs=in_specs, out_specs=out_specs, check_vma=False)
```

```python
import functools
import math

import jax
import jax.numpy as jnp
from jax import lax
from jax.experimental import pallas as pl
from jax.experimental.pallas import tpu as pltpu
from jax.sharding import PartitionSpec as P

MESH = pl.DeviceIdType.MESH

HEAD_SIZE = 128


rope_base = 1000000.0
neg_big = -1e30


def doc_number(token_positions, doc_ends):
    return jnp.sum((token_positions[:, None] >= doc_ends[None, :]).astype(jnp.int32), axis=1)


def whole_kernel(
    n, owners, chunks, presplit,
    x_ref, xq_ref, wq_ref, wk_ref, wv_ref, pack_ref, cot_ref,
    cos_ref, sin_ref, start_ref, choose_ref,
    att_ref, down_ref, up_ref,
    out_ref, held, xs, xq, packs, cot, ups, spread, low, mid, kv, bias, gq,
    give, got, keep, gath,
    load_sem, x_sem,
    up_send, down_send, y_send, core_send, z_recv, y_recv, core_recv,
    pack_send, pack_recv, low_send, low_recv, mid_send, mid_recv,
    kv_sem, got_sem, gath_send, gath_recv,
):
    depth = wq_ref.shape[0]
    row_count = xq.shape[0]
    query_cols = wq_ref.shape[1]
    key_cols = wk_ref.shape[1]
    rank = low.shape[1]
    o = lax.axis_index("owner")
    piece = depth // 4
    rows = piece // chunks
    g = lax.axis_index("groups")
    z = lax.axis_index("dp")
    s = lax.axis_index("seq")
    above = n - 1 - z
    below = z
    both = jnp.minimum(above, below)

    copies = []
    at = 0
    for i, ref in enumerate((wq_ref, wk_ref, wv_ref)):
        width = ref.shape[1]
        copies.append(
            pltpu.make_async_copy(ref, held.at[z, :, pl.ds(at, width)], load_sem.at[i])
        )
        at += width
    x_copies = []
    for d in range(n):
        src = x_ref.at[d] if presplit else x_ref.at[:, pl.ds(d * depth, depth)]
        x_copies.append(pltpu.make_async_copy(src, xs.at[d], x_sem.at[d]))
    width = xq.shape[1]
    x_copies.append(
        pltpu.make_async_copy(
            xq_ref.at[:, pl.ds(pl.multiple_of(o * width, 128), width)], xq, load_sem.at[3]
        )
    )
    x_copies.append(pltpu.make_async_copy(cot_ref, cot, load_sem.at[4]))
    copies.append(pltpu.make_async_copy(pack_ref, packs.at[z], load_sem.at[5]))
    for c in copies + x_copies:
        c.start()

    barrier = pltpu.get_barrier_semaphore()
    pl.semaphore_signal(barrier, inc=1, device_id={"groups": 1 - g}, device_id_type=MESH)
    pl.semaphore_signal(barrier, inc=1, device_id={"seq": 1 - s}, device_id_type=MESH)
    for k in range(1, n):
        pl.semaphore_signal(
            barrier, inc=1, device_id={"dp": lax.rem(z + k, n)}, device_id_type=MESH
        )
    for k in range(1, owners):
        pl.semaphore_signal(
            barrier, inc=1, device_id={"owner": lax.rem(o + k, owners)}, device_id_type=MESH
        )
    pl.semaphore_wait(barrier, n + owners)

    for c in copies:
        c.wait()

    def part(d, gg, ss, c):
        start = pl.multiple_of(((gg * 2 + ss) * chunks + c) * rows, 16)
        return held.at[d, pl.ds(start, rows), :]

    def move(d, gg, ss, c, send, recv, target):
        ref = part(d, gg, ss, c)
        return pltpu.make_async_remote_copy(
            src_ref=ref, dst_ref=ref, send_sem=send, recv_sem=recv,
            device_id=target, device_id_type=MESH,
        )

    def to_below(d, c):
        return move(d, g, s, c, down_send.at[d, c], z_recv.at[d, c], {"dp": jnp.maximum(z - 1, 0)})

    def to_above(d, c):
        return move(d, g, s, c, up_send.at[d, c], z_recv.at[d, c], {"dp": jnp.minimum(z + 1, n - 1)})

    def to_group(d, c):
        return move(d, g, s, c, y_send.at[d, c], y_recv.at[d, c], {"groups": 1 - g})

    def from_group(d, c):
        return move(d, 1 - g, s, c, y_send.at[d, c], y_recv.at[d, c], {"groups": 1 - g})

    def to_core(d, gg, c, k):
        return move(d, gg, s, c, core_send.at[d, c, k], core_recv.at[d, c, k], {"seq": 1 - s})

    def from_core(d, gg, c, k):
        return move(d, gg, 1 - s, c, core_send.at[d, c, k], core_recv.at[d, c, k], {"seq": 1 - s})

    def send_own(c):
        @pl.when(z > 0)
        def _():
            to_below(z, c).start()

        @pl.when(z < n - 1)
        def _():
            to_above(z, c).start()

    ahead = min(2, chunks)
    for c in range(ahead):
        send_own(c)
    pack_copies = [
        pltpu.make_async_remote_copy(
            src_ref=packs.at[z], dst_ref=packs.at[z],
            send_sem=pack_send.at[k], recv_sem=pack_recv.at[k],
            device_id={"dp": lax.rem(z + k, n)}, device_id_type=MESH,
        )
        for k in range(1, n)
    ]
    for c in pack_copies:
        c.start()
    for c in x_copies:
        c.wait()

    kpos = lax.broadcasted_iota(jnp.int32, bias.shape, 1)
    qpos = s * row_count + lax.broadcasted_iota(jnp.int32, bias.shape, 0)
    allowed = jnp.logical_and(kpos <= qpos, kpos >= start_ref[:, :1])
    bias[...] = jnp.where(allowed, 0.0, neg_big)

    def owner_copies(buf, send, recv):
        return [
            pltpu.make_async_remote_copy(
                src_ref=buf.at[0], dst_ref=buf.at[k],
                send_sem=send.at[k], recv_sem=recv.at[k],
                device_id={"owner": lax.rem(o + k, owners)}, device_id_type=MESH,
            )
            for k in range(1, owners)
        ]

    def chosen(wide):
        return jnp.sum((wide * choose_ref[...]).reshape(n, rank, row_count), axis=0)

    def spread_out(buf):
        total = buf[0]
        for k in range(1, owners):
            total = total + buf[k]
        total = total.astype(jnp.bfloat16).astype(jnp.float32)
        return (jnp.concatenate([total] * n, axis=0) * choose_ref[...]).astype(jnp.bfloat16)

    low_copies = owner_copies(low, low_send, low_recv)
    mid_copies = owner_copies(mid, mid_send, mid_recv)

    def low_first():
        for c in pack_copies:
            c.wait_recv()
        wide = packs[...].astype(jnp.float32)
        ups[...] = wide[:, :rank, :query_cols].reshape(n * rank, query_cols).astype(jnp.bfloat16)
        downs = jnp.concatenate([wide[:, :rank, query_cols:], wide[:, rank:, :]], axis=2)
        downs = downs.reshape(n * rank, width).astype(jnp.bfloat16)
        low[0] = chosen(
            lax.dot_general(
                downs, xq[...], (((1,), (1,)), ((), ())), preferred_element_type=jnp.float32
            )
        )
        for c in low_copies:
            c.start()

    def low_second():
        for c in low_copies:
            c.wait_recv()
        spread[...] = spread_out(low)

        def body(j, _):
            cols = pl.ds(pl.multiple_of(j * 256, 256), 256)
            out_ref[:, cols] += lax.dot_general(
                spread[...], ups[:, cols], (((0,), (0,)), ((), ())),
                preferred_element_type=jnp.float32,
            )
            return 0

        lax.fori_loop(0, query_cols // 256, body, 0)

    tile = 512
    tiles = out_ref.shape[1] // tile

    def multiply(d, first):
        def body(j, _):
            cols = pl.ds(pl.multiple_of(j * tile, tile), tile)
            term = jnp.dot(xs[d], held[d, :, cols], preferred_element_type=jnp.float32)
            if first:
                out_ref[:, cols] = term
            else:
                out_ref[:, cols] += term
            return 0

        lax.fori_loop(0, tiles, body, 0)

    multiply(z, True)

    def shard_of(k):
        paired = k < 2 * both
        half = k // 2
        single = jnp.where(above > below, z + 1 + (k - both), z - 1 - (k - both))
        return jnp.where(paired, jnp.where(k % 2 == 0, z + 1 + half, z - 1 - half), single)

    def event(i):
        paired = i < 2 * both * chunks
        t = i // 2
        t2 = i - both * chunks
        up = jnp.where(paired, i % 2 == 0, above > below)
        t = jnp.where(paired, t, t2)
        return jnp.where(up, z + 1 + t // chunks, z - 1 - t // chunks), t % chunks

    def land(d, c, onward, more):
        to_below(d, c).wait_recv()

        @pl.when(more)
        def _():
            onward(d, c).start()

        to_group(d, c).start()
        to_core(d, g, c, 0).start()

    lag = min(2, chunks - 1)

    def step(t, _):
        @pl.when(t + ahead < chunks)
        def _():
            send_own(jnp.minimum(t + ahead, chunks - 1))

        @pl.when(t < above * chunks)
        def _():
            land(jnp.minimum(z + 1 + t // chunks, n - 1), t % chunks, to_below, z > 0)

        @pl.when(t < below * chunks)
        def _():
            land(jnp.maximum(z - 1 - t // chunks, 0), t % chunks, to_above, z < n - 1)

        @pl.when(t >= lag)
        def _():
            cross(t - lag)

        return 0

    def cross(i):
        d, c = event(i)
        from_group(d, c).wait_recv()
        to_core(d, 1 - g, c, 1).start()

    def finish(k):
        d = shard_of(k)

        def body(c, _):
            from_core(d, g, c, 0).wait_recv()
            from_core(d, 1 - g, c, 1).wait_recv()
            return 0

        lax.fori_loop(0, chunks, body, 0)
        multiply(d, False)

    def phase(p, _):
        lax.fori_loop(p * chunks, (p + 1) * chunks, step, 0)

        @pl.when(p == 0)
        def _():
            low_first()

        @pl.when(p >= 2)
        def _():
            finish(jnp.maximum(p - 2, 0))

        return 0

    total = (n - 1) * chunks
    lax.fori_loop(0, n - 1, phase, 0)
    lax.fori_loop(total - lag, total, lambda i, _: (cross(i), 0)[1], 0)
    low_second()
    for k in range(max(n - 3, 0), n - 1):
        finish(jnp.int32(k))

    half = HEAD_SIZE // 2

    def rotate(v, direction):
        turned = pltpu.roll(v, half, 1) * sin_ref[...]
        return v * cos_ref[...] + (turned if direction > 0 else -turned)

    for c in range(key_cols // HEAD_SIZE):
        cols = pl.ds(c * HEAD_SIZE, HEAD_SIZE)
        raw = out_ref[:, pl.ds(query_cols + c * HEAD_SIZE, HEAD_SIZE)]
        kv[s, :, cols] = rotate(raw, 1).astype(jnp.bfloat16)
    kv[s, :, pl.ds(key_cols, key_cols)] = out_ref[
        :, pl.ds(query_cols + key_cols, key_cols)
    ].astype(jnp.bfloat16)
    kv_copy = pltpu.make_async_remote_copy(
        src_ref=kv.at[s], dst_ref=kv.at[s], send_sem=kv_sem.at[0], recv_sem=kv_sem.at[1],
        device_id={"seq": 1 - s}, device_id_type=MESH,
    )
    kv_copy.start()
    pltpu.make_async_remote_copy(
        src_ref=kv.at[1 - s], dst_ref=kv.at[1 - s], send_sem=kv_sem.at[0],
        recv_sem=kv_sem.at[1], device_id={"seq": 1 - s}, device_id_type=MESH,
    ).wait_recv()

    scale = 1.0 / math.sqrt(HEAD_SIZE)
    grouping = query_cols // key_cols

    def dot(a, b, da, db):
        return lax.dot_general(
            a, b, (((da,), (db,)), ((), ())), preferred_element_type=jnp.float32
        )

    def head(j, _):
        cols = pl.ds(pl.multiple_of(j * HEAD_SIZE, HEAD_SIZE), HEAD_SIZE)
        at = pl.multiple_of((j // grouping) * HEAD_SIZE, HEAD_SIZE)
        keys = kv[:, :, pl.ds(at, HEAD_SIZE)].reshape(2 * row_count, HEAD_SIZE)
        values = kv[:, :, pl.ds(at + key_cols, HEAD_SIZE)].reshape(2 * row_count, HEAD_SIZE)
        query = rotate(out_ref[:, cols], 1).astype(jnp.bfloat16)
        scores = dot(query, keys, 1, 1) * scale + bias[...]
        raised = jnp.exp(scores - jnp.max(scores, axis=1, keepdims=True))
        probability = raised * (1.0 / jnp.sum(raised, axis=1, keepdims=True))
        att_ref[:, cols] = dot(probability.astype(jnp.bfloat16), values, 1, 0).astype(
            jnp.bfloat16
        )
        dprob = dot(cot[:, cols], values, 1, 1)
        delta = jnp.sum(probability * dprob, axis=1, keepdims=True)
        dscore = (probability * (dprob - delta)).astype(jnp.bfloat16)
        gq[:, cols] = rotate(dot(dscore, keys, 1, 0) * scale, -1).astype(jnp.bfloat16)
        return 0

    lax.fori_loop(0, query_cols // HEAD_SIZE, head, 0)

    mid[0] = chosen(dot(ups[...], gq[...], 1, 1))
    for c in mid_copies:
        c.start()
    down_half = width // 2
    up_half = query_cols // 2

    def up_term(h):
        return dot(spread[...], gq[:, pl.ds(pl.multiple_of(h * up_half, 128), up_half)], 1, 0)

    def down_term(m, h):
        return dot(m, xq[:, pl.ds(pl.multiple_of(h * down_half, 128), down_half)], 1, 0)

    give[:, pl.ds(down_half, up_half)] = up_term(1 - s)
    for c in mid_copies:
        c.wait_recv()
    spread_mid = spread_out(mid)
    give[:, pl.ds(0, down_half)] = down_term(spread_mid, 1 - s)
    swap = pltpu.make_async_remote_copy(
        src_ref=give, dst_ref=got, send_sem=got_sem.at[0], recv_sem=got_sem.at[1],
        device_id={"seq": 1 - s}, device_id_type=MESH,
    )
    swap.start()
    mine_up = up_term(s)
    mine_down = down_term(spread_mid, s)
    swap.wait_recv()
    keep[:, :, pl.ds(0, down_half)] = (mine_down + got[:, pl.ds(0, down_half)]).reshape(
        n, rank, down_half
    )
    keep[:, :, pl.ds(down_half, up_half)] = (
        mine_up + got[:, pl.ds(down_half, up_half)]
    ).reshape(n, rank, up_half)
    gath_copies = [
        pltpu.make_async_remote_copy(
            src_ref=keep.at[lax.rem(z + k, n)], dst_ref=gath.at[k],
            send_sem=gath_send.at[k], recv_sem=gath_recv.at[k],
            device_id={"dp": lax.rem(z + k, n)}, device_id_type=MESH,
        )
        for k in range(1, n)
    ]
    for c in gath_copies:
        c.start()
    total_grad = keep[z]
    for k, c in enumerate(gath_copies):
        c.wait_recv()
        total_grad = total_grad + gath[k + 1]
    down_ref[...] = total_grad[:, :down_half]
    up_ref[...] = total_grad[:, down_half:]

    for c in pack_copies + low_copies + mid_copies + gath_copies + [kv_copy, swap]:
        c.wait_send()

    def drain(i, _):
        d = i // chunks
        c = i % chunks
        mine = d == z

        @pl.when(jnp.logical_and(d >= z, z > 0))
        def _():
            to_below(d, c).wait_send()

        @pl.when(jnp.logical_and(d <= z, z < n - 1))
        def _():
            to_above(d, c).wait_send()

        @pl.when(jnp.logical_not(mine))
        def _():
            to_group(d, c).wait_send()
            to_core(d, g, c, 0).wait_send()
            to_core(d, 1 - g, c, 1).wait_send()

        return 0

    lax.fori_loop(0, n * chunks, drain, 0)


def whole(
    tokens, query_weight, key_weight, value_weight, pack, cotangent, cosines, sines, starts, choose
):
    n = lax.axis_size("dp")
    owners = lax.axis_size("owner")
    row_count, width = tokens.shape
    depth, query_cols = query_weight.shape
    key_cols = key_weight.shape[1]
    cols = query_cols + 2 * key_cols
    wide = choose.shape[0]
    rank = wide // n
    quarter = width // owners
    summed = (quarter + query_cols) // 2
    piece = depth // 4
    chunks = max(c for c in range(1, 9) if piece % c == 0 and (piece // c) % 16 == 0)
    presplit = depth % 128 != 0
    split = tokens
    if presplit:
        split = jnp.transpose(tokens.reshape(row_count, n, depth), (1, 0, 2))
    dma = pltpu.SemaphoreType.DMA
    bf16 = jnp.bfloat16
    f32 = jnp.float32
    return pl.pallas_call(
        functools.partial(whole_kernel, n, owners, chunks, presplit),
        out_shape=(
            jax.ShapeDtypeStruct((row_count, query_cols), bf16),
            jax.ShapeDtypeStruct((rank, quarter // 2), f32),
            jax.ShapeDtypeStruct((rank, query_cols // 2), f32),
        ),
        in_specs=[pl.BlockSpec(memory_space=pl.ANY)] * 7
        + [pl.BlockSpec(memory_space=pltpu.VMEM)] * 4,
        out_specs=(pl.BlockSpec(memory_space=pltpu.VMEM),) * 3,
        scratch_shapes=[
            pltpu.VMEM((row_count, cols), f32),
            pltpu.VMEM((n, depth, cols), bf16),
            pltpu.VMEM((n, row_count, depth), bf16),
            pltpu.VMEM((row_count, quarter), bf16),
            pltpu.VMEM((n,) + pack.shape, bf16),
            pltpu.VMEM((row_count, query_cols), bf16),
            pltpu.VMEM((wide, query_cols), bf16),
            pltpu.VMEM((wide, row_count), bf16),
            pltpu.VMEM((owners, rank, row_count), f32),
            pltpu.VMEM((owners, rank, row_count), f32),
            pltpu.VMEM((2, row_count, 2 * key_cols), bf16),
            pltpu.VMEM((row_count, 2 * row_count), f32),
            pltpu.VMEM((row_count, query_cols), bf16),
            pltpu.VMEM((wide, summed), f32),
            pltpu.VMEM((wide, summed), f32),
            pltpu.VMEM((n, rank, summed), f32),
            pltpu.VMEM((n, rank, summed), f32),
            dma((6,)),
            dma((n,)),
            dma((n, chunks)),
            dma((n, chunks)),
            dma((n, chunks)),
            dma((n, chunks, 2)),
            dma((n, chunks)),
            dma((n, chunks)),
            dma((n, chunks, 2)),
            dma((n,)),
            dma((n,)),
            dma((owners,)),
            dma((owners,)),
            dma((owners,)),
            dma((owners,)),
            dma((2,)),
            dma((2,)),
            dma((n,)),
            dma((n,)),
        ],
        compiler_params=pltpu.CompilerParams(
            collective_id=0, has_side_effects=True, vmem_limit_bytes=56 * 2**20
        ),
        cost_estimate=pl.CostEstimate(
            flops=2 * row_count * n * depth * cols,
            bytes_accessed=2 * n * depth * cols,
            transcendentals=0,
        ),
    )(
        split, tokens, query_weight, key_weight, value_weight, pack, cotangent,
        cosines, sines, starts, choose,
    )


def shards(
    tokens,
    document_lengths,
    document_adapter,
    adapter_stored_row,
    query_weight,
    key_weight,
    value_weight,
    adapter_down_weight,
    adapter_up_weight,
    output_cotangent,
):
    row_count = tokens.shape[0]
    rank = adapter_down_weight.shape[2]
    adapters = lax.axis_size("dp")
    doc_count = document_lengths.shape[1]
    doc_ends = jnp.cumsum(document_lengths[0])
    own_positions = lax.axis_index("seq") * row_count + jnp.arange(row_count, dtype=jnp.int32)
    doc_mine = doc_number(own_positions, doc_ends)
    in_document = doc_mine[:, None] == jnp.arange(doc_count, dtype=jnp.int32)[None, :]
    starts = jnp.sum(jnp.where(in_document, (doc_ends - document_lengths[0])[None, :], 0), axis=1)
    starts = jnp.broadcast_to(starts[:, None], (row_count, HEAD_SIZE))
    adapter_of = jnp.sum(jnp.where(in_document, document_adapter[0][None, :], 0), axis=1)
    adapter_ids = jnp.arange(adapters, dtype=jnp.int32)
    stored_row = jnp.sum(
        jnp.where(adapter_of[:, None] == adapter_ids[None, :], adapter_stored_row[None, :], 0),
        axis=1,
    )
    row_of = jnp.arange(adapters * rank, dtype=jnp.int32) // rank
    choose = (row_of[:, None] == stored_row[None, :]).astype(jnp.float32)
    half_width = HEAD_SIZE // 2
    frequency = rope_base ** (
        -(jnp.arange(half_width).astype(jnp.float32) * 2.0 / HEAD_SIZE)
    )
    angles = own_positions.astype(jnp.float32)[:, None] * frequency[None, :]
    cosines = jnp.cos(angles)
    sines = jnp.sin(angles)
    cosines = jnp.concatenate([cosines, cosines], axis=1)
    sines = jnp.concatenate([-sines, sines], axis=1)
    line = jnp.concatenate([adapter_up_weight[0], jnp.transpose(adapter_down_weight[0])], axis=1)
    middle = line.shape[1] // 2
    pack = jnp.concatenate([line[:, :middle], line[:, middle:]], axis=0)
    attended, grad_down, grad_up = whole(
        tokens, query_weight, key_weight, value_weight, pack, output_cotangent,
        cosines, sines, starts, choose,
    )
    return (attended, jnp.transpose(grad_down)[None], grad_up[None])


def solution(mesh):
    in_specs = (
        P(("groups", "dp", "seq"), None),
        P(("groups", "dp"), None),
        P(("groups", "dp"), None),
        P(),
        P("dp", "owner"),
        P("dp", "owner"),
        P("dp", "owner"),
        P("dp", "owner", None),
        P("dp", None, "owner"),
        P(("groups", "dp", "seq"), "owner"),
    )
    out_specs = (
        P(("groups", "dp", "seq"), "owner"),
        P(("groups", "dp"), ("owner", "seq"), None),
        P(("groups", "dp"), None, ("owner", "seq")),
    )
    return jax.shard_map(shards, mesh=mesh, in_specs=in_specs, out_specs=out_specs, check_vma=False)
```

```python
import functools
import math

import jax
import jax.numpy as jnp
import numpy as np
from jax import lax
from jax.experimental import pallas as pl
from jax.experimental.pallas import tpu as pltpu
from jax.sharding import PartitionSpec as P

MESH = pl.DeviceIdType.MESH

HEAD_SIZE = 128


rope_base = 1000000.0
neg_big = -1e30


def whole_kernel(
    n, owners, chunks, presplit,
    x_ref, xq_ref, wq_ref, wk_ref, wv_ref, pack_ref, cot_ref,
    lengths_ref, adapters_ref, rows_ref, cos_hbm, sin_hbm,
    att_ref, down_ref, up_ref,
    out_ref, held, xs, xq, packs, cot, ups, spread, low, mid, kv, bias, gq,
    give, got, keep, gath, cos_ref, sin_ref, choose_ref,
    load_sem, x_sem,
    up_send, down_send, y_send, core_send, z_recv, y_recv, core_recv,
    pack_send, pack_recv, low_send, low_recv, mid_send, mid_recv,
    kv_sem, got_sem, gath_send, gath_recv,
):
    depth = wq_ref.shape[0]
    row_count = xq.shape[0]
    query_cols = wq_ref.shape[1]
    key_cols = wk_ref.shape[1]
    rank = low.shape[1]
    o = lax.axis_index("owner")
    piece = depth // 4
    rows = piece // chunks
    g = lax.axis_index("groups")
    z = lax.axis_index("dp")
    s = lax.axis_index("seq")
    above = n - 1 - z
    below = z
    both = jnp.minimum(above, below)

    copies = []
    at = 0
    for i, ref in enumerate((wq_ref, wk_ref, wv_ref)):
        width = ref.shape[1]
        copies.append(
            pltpu.make_async_copy(ref, held.at[z, :, pl.ds(at, width)], load_sem.at[i])
        )
        at += width
    x_copies = []
    for d in range(n):
        src = x_ref.at[d] if presplit else x_ref.at[:, pl.ds(d * depth, depth)]
        x_copies.append(pltpu.make_async_copy(src, xs.at[d], x_sem.at[d]))
    width = xq.shape[1]
    x_copies.append(
        pltpu.make_async_copy(
            xq_ref.at[:, pl.ds(pl.multiple_of(o * width, 128), width)], xq, load_sem.at[3]
        )
    )
    x_copies.append(pltpu.make_async_copy(cot_ref, cot, load_sem.at[4]))
    for i, (src, dst) in enumerate(((cos_hbm, cos_ref), (sin_hbm, sin_ref))):
        first = pl.multiple_of(s * row_count, 8)
        x_copies.append(
            pltpu.make_async_copy(src.at[pl.ds(first, row_count), :], dst, load_sem.at[6 + i])
        )
    copies.append(pltpu.make_async_copy(pack_ref, packs.at[z], load_sem.at[5]))
    for c in copies + x_copies:
        c.start()

    barrier = pltpu.get_barrier_semaphore()
    pl.semaphore_signal(barrier, inc=1, device_id={"groups": 1 - g}, device_id_type=MESH)
    pl.semaphore_signal(barrier, inc=1, device_id={"seq": 1 - s}, device_id_type=MESH)
    for k in range(1, n):
        pl.semaphore_signal(
            barrier, inc=1, device_id={"dp": lax.rem(z + k, n)}, device_id_type=MESH
        )
    for k in range(1, owners):
        pl.semaphore_signal(
            barrier, inc=1, device_id={"owner": lax.rem(o + k, owners)}, device_id_type=MESH
        )
    pl.semaphore_wait(barrier, n + owners)

    for c in copies:
        c.wait()

    def part(d, gg, ss, c):
        start = pl.multiple_of(((gg * 2 + ss) * chunks + c) * rows, 16)
        return held.at[d, pl.ds(start, rows), :]

    def move(d, gg, ss, c, send, recv, target):
        ref = part(d, gg, ss, c)
        return pltpu.make_async_remote_copy(
            src_ref=ref, dst_ref=ref, send_sem=send, recv_sem=recv,
            device_id=target, device_id_type=MESH,
        )

    def to_below(d, c):
        return move(d, g, s, c, down_send.at[d, c], z_recv.at[d, c], {"dp": jnp.maximum(z - 1, 0)})

    def to_above(d, c):
        return move(d, g, s, c, up_send.at[d, c], z_recv.at[d, c], {"dp": jnp.minimum(z + 1, n - 1)})

    def to_group(d, c):
        return move(d, g, s, c, y_send.at[d, c], y_recv.at[d, c], {"groups": 1 - g})

    def from_group(d, c):
        return move(d, 1 - g, s, c, y_send.at[d, c], y_recv.at[d, c], {"groups": 1 - g})

    def to_core(d, gg, c, k):
        return move(d, gg, s, c, core_send.at[d, c, k], core_recv.at[d, c, k], {"seq": 1 - s})

    def from_core(d, gg, c, k):
        return move(d, gg, 1 - s, c, core_send.at[d, c, k], core_recv.at[d, c, k], {"seq": 1 - s})

    def send_down(t):
        @pl.when(jnp.logical_and(z > 0, t < (above + 1) * chunks))
        def _():
            to_below(jnp.minimum(z + t // chunks, n - 1), t % chunks).start()

    def send_up(t):
        @pl.when(jnp.logical_and(z < n - 1, t < (below + 1) * chunks))
        def _():
            to_above(jnp.maximum(z - t // chunks, 0), t % chunks).start()

    ahead = min(2, chunks)
    for t in range(ahead):
        send_down(t)
        send_up(t)
    pack_copies = [
        pltpu.make_async_remote_copy(
            src_ref=packs.at[z], dst_ref=packs.at[z],
            send_sem=pack_send.at[k], recv_sem=pack_recv.at[k],
            device_id={"dp": lax.rem(z + k, n)}, device_id_type=MESH,
        )
        for k in range(1, n)
    ]
    for c in pack_copies:
        c.start()
    for c in x_copies:
        c.wait()

    kpos = lax.broadcasted_iota(jnp.int32, bias.shape, 1)
    qpos = s * row_count + lax.broadcasted_iota(jnp.int32, bias.shape, 0)
    tpos = s * row_count + lax.broadcasted_iota(jnp.int32, choose_ref.shape, 1)
    begin = jnp.zeros(bias.shape, jnp.int32)
    stored = jnp.zeros(choose_ref.shape, jnp.int32)
    end = jnp.int32(0)
    for doc in range(lengths_ref.shape[1]):
        adapter = adapters_ref[0, doc]
        row = jnp.int32(0)
        for i in range(rows_ref.shape[0]):
            row = row + jnp.where(adapter == i, rows_ref[i], 0)
        begin = jnp.where(qpos >= end, end, begin)
        stored = jnp.where(tpos >= end, row, stored)
        end = end + lengths_ref[0, doc]
    row_of = lax.broadcasted_iota(jnp.int32, choose_ref.shape, 0) // rank
    choose_ref[...] = jnp.where(row_of == stored, 1.0, 0.0)
    allowed = jnp.logical_and(kpos <= qpos, kpos >= begin)
    bias[...] = jnp.where(allowed, 0.0, neg_big)

    def owner_copies(buf, send, recv):
        return [
            pltpu.make_async_remote_copy(
                src_ref=buf.at[0], dst_ref=buf.at[k],
                send_sem=send.at[k], recv_sem=recv.at[k],
                device_id={"owner": lax.rem(o + k, owners)}, device_id_type=MESH,
            )
            for k in range(1, owners)
        ]

    def chosen(wide):
        return jnp.sum((wide * choose_ref[...]).reshape(n, rank, row_count), axis=0)

    def spread_out(buf):
        total = buf[0]
        for k in range(1, owners):
            total = total + buf[k]
        total = total.astype(jnp.bfloat16).astype(jnp.float32)
        return (jnp.concatenate([total] * n, axis=0) * choose_ref[...]).astype(jnp.bfloat16)

    low_copies = owner_copies(low, low_send, low_recv)
    mid_copies = owner_copies(mid, mid_send, mid_recv)

    def low_first():
        for c in pack_copies:
            c.wait_recv()
        wide = packs[...].astype(jnp.float32)
        ups[...] = wide[:, :rank, :query_cols].reshape(n * rank, query_cols).astype(jnp.bfloat16)
        downs = jnp.concatenate([wide[:, :rank, query_cols:], wide[:, rank:, :]], axis=2)
        downs = downs.reshape(n * rank, width).astype(jnp.bfloat16)
        low[0] = chosen(
            lax.dot_general(
                downs, xq[...], (((1,), (1,)), ((), ())), preferred_element_type=jnp.float32
            )
        )
        for c in low_copies:
            c.start()

    def low_second():
        for c in low_copies:
            c.wait_recv()
        spread[...] = spread_out(low)

        def body(j, _):
            cols = pl.ds(pl.multiple_of(j * 256, 256), 256)
            out_ref[:, cols] += lax.dot_general(
                spread[...], ups[:, cols], (((0,), (0,)), ((), ())),
                preferred_element_type=jnp.float32,
            )
            return 0

        lax.fori_loop(0, query_cols // 256, body, 0)

    tile = 512
    tiles = out_ref.shape[1] // tile

    def multiply(d, first):
        def body(j, _):
            cols = pl.ds(pl.multiple_of(j * tile, tile), tile)
            term = jnp.dot(xs[d], held[d, :, cols], preferred_element_type=jnp.float32)
            if first:
                out_ref[:, cols] = term
            else:
                out_ref[:, cols] += term
            return 0

        lax.fori_loop(0, tiles, body, 0)

    multiply(z, True)

    def shard_of(k):
        paired = k < 2 * both
        half = k // 2
        single = jnp.where(above > below, z + 1 + (k - both), z - 1 - (k - both))
        return jnp.where(paired, jnp.where(k % 2 == 0, z + 1 + half, z - 1 - half), single)

    def event(i):
        paired = i < 2 * both * chunks
        t = i // 2
        t2 = i - both * chunks
        up = jnp.where(paired, i % 2 == 0, above > below)
        t = jnp.where(paired, t, t2)
        return jnp.where(up, z + 1 + t // chunks, z - 1 - t // chunks), t % chunks

    def land(d, c):
        to_below(d, c).wait_recv()
        to_core(d, g, c, 0).start()

    lag = min(3, chunks - 1)

    def step(t, _):
        @pl.when(t < above * chunks)
        def _():
            land(jnp.minimum(z + 1 + t // chunks, n - 1), t % chunks)

        @pl.when(t < below * chunks)
        def _():
            land(jnp.maximum(z - 1 - t // chunks, 0), t % chunks)

        send_down(t + ahead)
        send_up(t + ahead)
        to_group(*event(t)).start()

        @pl.when(t >= lag)
        def _():
            cross(t - lag)

        return 0

    def cross(i):
        d, c = event(i)
        from_group(d, c).wait_recv()
        to_core(d, 1 - g, c, 1).start()

    def finish(k):
        d = shard_of(k)

        def body(c, _):
            from_core(d, g, c, 0).wait_recv()
            from_core(d, 1 - g, c, 1).wait_recv()
            return 0

        lax.fori_loop(0, chunks, body, 0)
        multiply(d, False)

    def phase(p, _):
        lax.fori_loop(p * chunks, (p + 1) * chunks, step, 0)

        @pl.when(p == 0)
        def _():
            low_first()

        @pl.when(p >= 2)
        def _():
            finish(jnp.maximum(p - 2, 0))

        return 0

    total = (n - 1) * chunks
    lax.fori_loop(0, n - 1, phase, 0)
    lax.fori_loop(total - lag, total, lambda i, _: (cross(i), 0)[1], 0)
    low_second()
    for k in range(max(n - 3, 0), n - 1):
        finish(jnp.int32(k))

    half = HEAD_SIZE // 2

    def rotate(v, direction):
        turned = pltpu.roll(v, half, 1) * sin_ref[...]
        return v * cos_ref[...] + (turned if direction > 0 else -turned)

    for c in range(key_cols // HEAD_SIZE):
        cols = pl.ds(c * HEAD_SIZE, HEAD_SIZE)
        raw = out_ref[:, pl.ds(query_cols + c * HEAD_SIZE, HEAD_SIZE)]
        kv[s, :, cols] = rotate(raw, 1).astype(jnp.bfloat16)
    kv[s, :, pl.ds(key_cols, key_cols)] = out_ref[
        :, pl.ds(query_cols + key_cols, key_cols)
    ].astype(jnp.bfloat16)
    kv_copy = pltpu.make_async_remote_copy(
        src_ref=kv.at[s], dst_ref=kv.at[s], send_sem=kv_sem.at[0], recv_sem=kv_sem.at[1],
        device_id={"seq": 1 - s}, device_id_type=MESH,
    )
    kv_copy.start()
    pltpu.make_async_remote_copy(
        src_ref=kv.at[1 - s], dst_ref=kv.at[1 - s], send_sem=kv_sem.at[0],
        recv_sem=kv_sem.at[1], device_id={"seq": 1 - s}, device_id_type=MESH,
    ).wait_recv()

    scale = 1.0 / math.sqrt(HEAD_SIZE)
    grouping = query_cols // key_cols

    def dot(a, b, da, db):
        return lax.dot_general(
            a, b, (((da,), (db,)), ((), ())), preferred_element_type=jnp.float32
        )

    def head(j, _):
        cols = pl.ds(pl.multiple_of(j * HEAD_SIZE, HEAD_SIZE), HEAD_SIZE)
        at = pl.multiple_of((j // grouping) * HEAD_SIZE, HEAD_SIZE)
        keys = kv[:, :, pl.ds(at, HEAD_SIZE)].reshape(2 * row_count, HEAD_SIZE)
        values = kv[:, :, pl.ds(at + key_cols, HEAD_SIZE)].reshape(2 * row_count, HEAD_SIZE)
        query = rotate(out_ref[:, cols], 1).astype(jnp.bfloat16)
        scores = dot(query, keys, 1, 1) * scale + bias[...]
        raised = jnp.exp(scores - jnp.max(scores, axis=1, keepdims=True))
        probability = raised * (1.0 / jnp.sum(raised, axis=1, keepdims=True))
        att_ref[:, cols] = dot(probability.astype(jnp.bfloat16), values, 1, 0).astype(
            jnp.bfloat16
        )
        dprob = dot(cot[:, cols], values, 1, 1)
        delta = jnp.sum(probability * dprob, axis=1, keepdims=True)
        dscore = (probability * (dprob - delta)).astype(jnp.bfloat16)
        gq[:, cols] = rotate(dot(dscore, keys, 1, 0) * scale, -1).astype(jnp.bfloat16)
        return 0

    lax.fori_loop(0, query_cols // HEAD_SIZE, head, 0)

    mid[0] = chosen(dot(ups[...], gq[...], 1, 1))
    for c in mid_copies:
        c.start()
    down_half = width // 2
    up_half = query_cols // 2

    def up_term(h):
        return dot(spread[...], gq[:, pl.ds(pl.multiple_of(h * up_half, 128), up_half)], 1, 0)

    def down_term(m, h):
        return dot(m, xq[:, pl.ds(pl.multiple_of(h * down_half, 128), down_half)], 1, 0)

    give[:, pl.ds(down_half, up_half)] = up_term(1 - s)
    for c in mid_copies:
        c.wait_recv()
    spread_mid = spread_out(mid)
    give[:, pl.ds(0, down_half)] = down_term(spread_mid, 1 - s)
    swap = pltpu.make_async_remote_copy(
        src_ref=give, dst_ref=got, send_sem=got_sem.at[0], recv_sem=got_sem.at[1],
        device_id={"seq": 1 - s}, device_id_type=MESH,
    )
    swap.start()
    mine_up = up_term(s)
    mine_down = down_term(spread_mid, s)
    swap.wait_recv()
    keep[:, :, pl.ds(0, down_half)] = (mine_down + got[:, pl.ds(0, down_half)]).reshape(
        n, rank, down_half
    )
    keep[:, :, pl.ds(down_half, up_half)] = (
        mine_up + got[:, pl.ds(down_half, up_half)]
    ).reshape(n, rank, up_half)
    gath_copies = [
        pltpu.make_async_remote_copy(
            src_ref=keep.at[lax.rem(z + k, n)], dst_ref=gath.at[k],
            send_sem=gath_send.at[k], recv_sem=gath_recv.at[k],
            device_id={"dp": lax.rem(z + k, n)}, device_id_type=MESH,
        )
        for k in range(1, n)
    ]
    for c in gath_copies:
        c.start()
    total_grad = keep[z]
    for k, c in enumerate(gath_copies):
        c.wait_recv()
        total_grad = total_grad + gath[k + 1]
    down_ref[...] = total_grad[:, :down_half]
    up_ref[...] = total_grad[:, down_half:]

    for c in pack_copies + low_copies + mid_copies + gath_copies + [kv_copy, swap]:
        c.wait_send()

    def drain(i, _):
        d = i // chunks
        c = i % chunks
        mine = d == z

        @pl.when(jnp.logical_and(d >= z, z > 0))
        def _():
            to_below(d, c).wait_send()

        @pl.when(jnp.logical_and(d <= z, z < n - 1))
        def _():
            to_above(d, c).wait_send()

        @pl.when(jnp.logical_not(mine))
        def _():
            to_group(d, c).wait_send()
            to_core(d, g, c, 0).wait_send()
            to_core(d, 1 - g, c, 1).wait_send()

        return 0

    lax.fori_loop(0, n * chunks, drain, 0)


def whole(
    tokens, query_weight, key_weight, value_weight, pack, cotangent, lengths, adapters, rows
):
    n = lax.axis_size("dp")
    owners = lax.axis_size("owner")
    row_count, width = tokens.shape
    depth, query_cols = query_weight.shape
    key_cols = key_weight.shape[1]
    cols = query_cols + 2 * key_cols
    rank = pack.shape[0] // 2
    wide = n * rank
    quarter = width // owners
    summed = (quarter + query_cols) // 2
    piece = depth // 4
    chunks = max(c for c in range(1, 9) if piece % c == 0 and (piece // c) % 16 == 0)
    presplit = depth % 128 != 0
    split = tokens
    if presplit:
        split = jnp.transpose(tokens.reshape(row_count, n, depth), (1, 0, 2))
    length = 2 * row_count
    angles = np.arange(length)[:, None] * rope_base ** (
        -np.arange(HEAD_SIZE // 2)[None, :] * 2.0 / HEAD_SIZE
    )
    cosines = np.concatenate([np.cos(angles), np.cos(angles)], axis=1).astype(np.float32)
    sines = np.concatenate([-np.sin(angles), np.sin(angles)], axis=1).astype(np.float32)
    dma = pltpu.SemaphoreType.DMA
    bf16 = jnp.bfloat16
    f32 = jnp.float32
    return pl.pallas_call(
        functools.partial(whole_kernel, n, owners, chunks, presplit),
        out_shape=(
            jax.ShapeDtypeStruct((row_count, query_cols), bf16),
            jax.ShapeDtypeStruct((rank, quarter // 2), f32),
            jax.ShapeDtypeStruct((rank, query_cols // 2), f32),
        ),
        in_specs=[pl.BlockSpec(memory_space=pl.ANY)] * 7
        + [pl.BlockSpec(memory_space=pltpu.SMEM)] * 3
        + [pl.BlockSpec(memory_space=pl.ANY)] * 2,
        out_specs=(pl.BlockSpec(memory_space=pltpu.VMEM),) * 3,
        scratch_shapes=[
            pltpu.VMEM((row_count, cols), f32),
            pltpu.VMEM((n, depth, cols), bf16),
            pltpu.VMEM((n, row_count, depth), bf16),
            pltpu.VMEM((row_count, quarter), bf16),
            pltpu.VMEM((n,) + pack.shape, bf16),
            pltpu.VMEM((row_count, query_cols), bf16),
            pltpu.VMEM((wide, query_cols), bf16),
            pltpu.VMEM((wide, row_count), bf16),
            pltpu.VMEM((owners, rank, row_count), f32),
            pltpu.VMEM((owners, rank, row_count), f32),
            pltpu.VMEM((2, row_count, 2 * key_cols), bf16),
            pltpu.VMEM((row_count, 2 * row_count), f32),
            pltpu.VMEM((row_count, query_cols), bf16),
            pltpu.VMEM((wide, summed), f32),
            pltpu.VMEM((wide, summed), f32),
            pltpu.VMEM((n, rank, summed), f32),
            pltpu.VMEM((n, rank, summed), f32),
            pltpu.VMEM((row_count, HEAD_SIZE), f32),
            pltpu.VMEM((row_count, HEAD_SIZE), f32),
            pltpu.VMEM((wide, row_count), f32),
            dma((8,)),
            dma((n,)),
            dma((n, chunks)),
            dma((n, chunks)),
            dma((n, chunks)),
            dma((n, chunks, 2)),
            dma((n, chunks)),
            dma((n, chunks)),
            dma((n, chunks, 2)),
            dma((n,)),
            dma((n,)),
            dma((owners,)),
            dma((owners,)),
            dma((owners,)),
            dma((owners,)),
            dma((2,)),
            dma((2,)),
            dma((n,)),
            dma((n,)),
        ],
        compiler_params=pltpu.CompilerParams(
            collective_id=0, has_side_effects=True, vmem_limit_bytes=56 * 2**20
        ),
        cost_estimate=pl.CostEstimate(
            flops=2 * row_count * n * depth * cols,
            bytes_accessed=2 * n * depth * cols,
            transcendentals=0,
        ),
    )(
        split, tokens, query_weight, key_weight, value_weight, pack, cotangent,
        lengths, adapters, rows, jnp.asarray(cosines), jnp.asarray(sines),
    )


def shards(
    tokens,
    document_lengths,
    document_adapter,
    adapter_stored_row,
    query_weight,
    key_weight,
    value_weight,
    adapter_down_weight,
    adapter_up_weight,
    output_cotangent,
):
    line = jnp.concatenate([adapter_up_weight[0], jnp.transpose(adapter_down_weight[0])], axis=1)
    middle = line.shape[1] // 2
    pack = jnp.concatenate([line[:, :middle], line[:, middle:]], axis=0)
    attended, grad_down, grad_up = whole(
        tokens, query_weight, key_weight, value_weight, pack, output_cotangent,
        document_lengths, document_adapter, adapter_stored_row,
    )
    return (attended, jnp.transpose(grad_down)[None], grad_up[None])


def solution(mesh):
    in_specs = (
        P(("groups", "dp", "seq"), None),
        P(("groups", "dp"), None),
        P(("groups", "dp"), None),
        P(),
        P("dp", "owner"),
        P("dp", "owner"),
        P("dp", "owner"),
        P("dp", "owner", None),
        P("dp", None, "owner"),
        P(("groups", "dp", "seq"), "owner"),
    )
    out_specs = (
        P(("groups", "dp", "seq"), "owner"),
        P(("groups", "dp"), ("owner", "seq"), None),
        P(("groups", "dp"), None, ("owner", "seq")),
    )
    return jax.shard_map(shards, mesh=mesh, in_specs=in_specs, out_specs=out_specs, check_vma=False)
```

```python
import functools
import math

import jax
import jax.numpy as jnp
import numpy as np
from jax import lax
from jax.experimental import pallas as pl
from jax.experimental.pallas import tpu as pltpu
from jax.sharding import PartitionSpec as P

MESH = pl.DeviceIdType.MESH

HEAD_SIZE = 128


rope_base = 1000000.0
neg_big = -1e30


def whole_kernel(
    n, owners, chunks, presplit,
    x_ref, xq_ref, wq_ref, wk_ref, wv_ref, pack_ref, cot_ref,
    lengths_ref, adapters_ref, rows_ref, cos_hbm, sin_hbm,
    att_ref, down_ref, up_ref,
    out_ref, held, xs, xq, packs, cot, ups, spread, low, mid, kv, bias, gq,
    give, got, keep, gath, cos_ref, sin_ref, choose_ref,
    load_sem, x_sem,
    up_send, down_send, y_send, core_send, z_recv, y_recv, core_recv,
    pack_send, pack_recv, pack_out, pack_in, low_send, low_recv, mid_send, mid_recv,
    kv_sem, got_sem, gath_send, gath_recv,
):
    depth = wq_ref.shape[0]
    row_count = xq.shape[0]
    query_cols = wq_ref.shape[1]
    key_cols = wk_ref.shape[1]
    rank = low.shape[1]
    o = lax.axis_index("owner")
    piece = depth // 4
    rows = piece // chunks
    g = lax.axis_index("groups")
    z = lax.axis_index("dp")
    s = lax.axis_index("seq")
    above = n - 1 - z
    below = z
    both = jnp.minimum(above, below)

    copies = []
    at = 0
    for i, ref in enumerate((wq_ref, wk_ref, wv_ref)):
        width = ref.shape[1]
        copies.append(
            pltpu.make_async_copy(ref, held.at[z, :, pl.ds(at, width)], load_sem.at[i])
        )
        at += width
    x_copies = []
    for d in range(n):
        src = x_ref.at[d] if presplit else x_ref.at[:, pl.ds(d * depth, depth)]
        x_copies.append(pltpu.make_async_copy(src, xs.at[d], x_sem.at[d]))
    width = xq.shape[1]
    x_copies.append(
        pltpu.make_async_copy(
            xq_ref.at[:, pl.ds(pl.multiple_of(o * width, 128), width)], xq, load_sem.at[3]
        )
    )
    x_copies.append(pltpu.make_async_copy(cot_ref, cot, load_sem.at[4]))
    for i, (src, dst) in enumerate(((cos_hbm, cos_ref), (sin_hbm, sin_ref))):
        first = pl.multiple_of(s * row_count, 8)
        x_copies.append(
            pltpu.make_async_copy(src.at[pl.ds(first, row_count), :], dst, load_sem.at[6 + i])
        )
    copies.append(pltpu.make_async_copy(pack_ref, packs.at[z], load_sem.at[5]))
    for c in copies + x_copies:
        c.start()

    barrier = pltpu.get_barrier_semaphore()
    pl.semaphore_signal(barrier, inc=1, device_id={"groups": 1 - g}, device_id_type=MESH)
    pl.semaphore_signal(barrier, inc=1, device_id={"seq": 1 - s}, device_id_type=MESH)
    for k in range(1, n):
        pl.semaphore_signal(
            barrier, inc=1, device_id={"dp": lax.rem(z + k, n)}, device_id_type=MESH
        )
    for k in range(1, owners):
        pl.semaphore_signal(
            barrier, inc=1, device_id={"owner": lax.rem(o + k, owners)}, device_id_type=MESH
        )
    pl.semaphore_wait(barrier, n + owners)

    for c in copies:
        c.wait()

    def part(d, gg, ss, c):
        start = pl.multiple_of(((gg * 2 + ss) * chunks + c) * rows, 16)
        return held.at[d, pl.ds(start, rows), :]

    def move(d, gg, ss, c, send, recv, target):
        ref = part(d, gg, ss, c)
        return pltpu.make_async_remote_copy(
            src_ref=ref, dst_ref=ref, send_sem=send, recv_sem=recv,
            device_id=target, device_id_type=MESH,
        )

    def to_below(d, c):
        return move(d, g, s, c, down_send.at[d, c], z_recv.at[d, c], {"dp": jnp.maximum(z - 1, 0)})

    def to_above(d, c):
        return move(d, g, s, c, up_send.at[d, c], z_recv.at[d, c], {"dp": jnp.minimum(z + 1, n - 1)})

    def to_group(d, c):
        return move(d, g, s, c, y_send.at[d, c], y_recv.at[d, c], {"groups": 1 - g})

    def from_group(d, c):
        return move(d, 1 - g, s, c, y_send.at[d, c], y_recv.at[d, c], {"groups": 1 - g})

    def to_core(d, gg, c, k):
        return move(d, gg, s, c, core_send.at[d, c, k], core_recv.at[d, c, k], {"seq": 1 - s})

    def from_core(d, gg, c, k):
        return move(d, gg, 1 - s, c, core_send.at[d, c, k], core_recv.at[d, c, k], {"seq": 1 - s})

    def send_down(t):
        @pl.when(jnp.logical_and(z > 0, t < (above + 1) * chunks))
        def _():
            to_below(jnp.minimum(z + t // chunks, n - 1), t % chunks).start()

    def send_up(t):
        @pl.when(jnp.logical_and(z < n - 1, t < (below + 1) * chunks))
        def _():
            to_above(jnp.maximum(z - t // chunks, 0), t % chunks).start()

    ahead = min(2, chunks)
    for t in range(ahead):
        send_down(t)
        send_up(t)
    pack_half = packs.shape[2] // 2

    def pack_part(d, ss):
        return packs.at[d, :, pl.ds(pl.multiple_of(ss * pack_half, 128), pack_half)]

    pack_copies = [
        pltpu.make_async_remote_copy(
            src_ref=pack_part(z, s), dst_ref=pack_part(z, s),
            send_sem=pack_send.at[k], recv_sem=pack_recv.at[k],
            device_id={"dp": lax.rem(z + k, n)}, device_id_type=MESH,
        )
        for k in range(1, n)
    ]

    def pack_swap(k, ss):
        d = lax.rem(z - k + n, n)
        return pltpu.make_async_remote_copy(
            src_ref=pack_part(d, ss), dst_ref=pack_part(d, ss),
            send_sem=pack_out.at[k], recv_sem=pack_in.at[k],
            device_id={"seq": 1 - s}, device_id_type=MESH,
        )

    for c in pack_copies:
        c.start()
    for c in x_copies:
        c.wait()

    kpos = lax.broadcasted_iota(jnp.int32, bias.shape, 1)
    qpos = s * row_count + lax.broadcasted_iota(jnp.int32, bias.shape, 0)
    tpos = s * row_count + lax.broadcasted_iota(jnp.int32, choose_ref.shape, 1)
    begin = jnp.zeros(bias.shape, jnp.int32)
    stored = jnp.zeros(choose_ref.shape, jnp.int32)
    end = jnp.int32(0)
    for doc in range(lengths_ref.shape[1]):
        adapter = adapters_ref[0, doc]
        row = jnp.int32(0)
        for i in range(rows_ref.shape[0]):
            row = row + jnp.where(adapter == i, rows_ref[i], 0)
        begin = jnp.where(qpos >= end, end, begin)
        stored = jnp.where(tpos >= end, row, stored)
        end = end + lengths_ref[0, doc]
    row_of = lax.broadcasted_iota(jnp.int32, choose_ref.shape, 0) // rank
    choose_ref[...] = jnp.where(row_of == stored, 1.0, 0.0)
    allowed = jnp.logical_and(kpos <= qpos, kpos >= begin)
    bias[...] = jnp.where(allowed, 0.0, neg_big)

    def owner_copies(buf, send, recv):
        return [
            pltpu.make_async_remote_copy(
                src_ref=buf.at[0], dst_ref=buf.at[k],
                send_sem=send.at[k], recv_sem=recv.at[k],
                device_id={"owner": lax.rem(o + k, owners)}, device_id_type=MESH,
            )
            for k in range(1, owners)
        ]

    def chosen(wide):
        return jnp.sum((wide * choose_ref[...]).reshape(n, rank, row_count), axis=0)

    def spread_out(buf):
        total = buf[0]
        for k in range(1, owners):
            total = total + buf[k]
        total = total.astype(jnp.bfloat16).astype(jnp.float32)
        return (jnp.concatenate([total] * n, axis=0) * choose_ref[...]).astype(jnp.bfloat16)

    low_copies = owner_copies(low, low_send, low_recv)
    mid_copies = owner_copies(mid, mid_send, mid_recv)

    def low_first():
        for k, c in enumerate(pack_copies):
            c.wait_recv()
            pack_swap(k + 1, s).start()
        for k in range(1, n):
            pack_swap(k, 1 - s).wait_recv()
        wide = packs[:, :, : (query_cols + width) // 2].astype(jnp.float32)
        ups[...] = wide[:, :rank, :query_cols].reshape(n * rank, query_cols).astype(jnp.bfloat16)
        downs = jnp.concatenate([wide[:, :rank, query_cols:], wide[:, rank:, :]], axis=2)
        downs = downs.reshape(n * rank, width).astype(jnp.bfloat16)
        low[0] = chosen(
            lax.dot_general(
                downs, xq[...], (((1,), (1,)), ((), ())), preferred_element_type=jnp.float32
            )
        )
        for c in low_copies:
            c.start()

    def low_second():
        for c in low_copies:
            c.wait_recv()
        spread[...] = spread_out(low)

        def body(j, _):
            cols = pl.ds(pl.multiple_of(j * 256, 256), 256)
            out_ref[:, cols] += lax.dot_general(
                spread[...], ups[:, cols], (((0,), (0,)), ((), ())),
                preferred_element_type=jnp.float32,
            )
            return 0

        lax.fori_loop(0, query_cols // 256, body, 0)

    tile = 512
    tiles = out_ref.shape[1] // tile

    def multiply(d, first):
        def body(j, _):
            cols = pl.ds(pl.multiple_of(j * tile, tile), tile)
            term = jnp.dot(xs[d], held[d, :, cols], preferred_element_type=jnp.float32)
            if first:
                out_ref[:, cols] = term
            else:
                out_ref[:, cols] += term
            return 0

        lax.fori_loop(0, tiles, body, 0)

    multiply(z, True)

    def shard_of(k):
        paired = k < 2 * both
        half = k // 2
        single = jnp.where(above > below, z + 1 + (k - both), z - 1 - (k - both))
        return jnp.where(paired, jnp.where(k % 2 == 0, z + 1 + half, z - 1 - half), single)

    def event(i):
        paired = i < 2 * both * chunks
        t = i // 2
        t2 = i - both * chunks
        up = jnp.where(paired, i % 2 == 0, above > below)
        t = jnp.where(paired, t, t2)
        return jnp.where(up, z + 1 + t // chunks, z - 1 - t // chunks), t % chunks

    def land(d, c):
        to_below(d, c).wait_recv()
        to_core(d, g, c, 0).start()

    lag = min(3, chunks - 1)

    def step(t, _):
        @pl.when(t < above * chunks)
        def _():
            land(jnp.minimum(z + 1 + t // chunks, n - 1), t % chunks)

        @pl.when(t < below * chunks)
        def _():
            land(jnp.maximum(z - 1 - t // chunks, 0), t % chunks)

        send_down(t + ahead)
        send_up(t + ahead)
        to_group(*event(t)).start()

        @pl.when(t >= lag)
        def _():
            cross(t - lag)

        return 0

    def cross(i):
        d, c = event(i)
        from_group(d, c).wait_recv()
        to_core(d, 1 - g, c, 1).start()

    def finish(k):
        d = shard_of(k)

        def body(c, _):
            from_core(d, g, c, 0).wait_recv()
            from_core(d, 1 - g, c, 1).wait_recv()
            return 0

        lax.fori_loop(0, chunks, body, 0)
        multiply(d, False)

    def phase(p, _):
        middle = p * chunks + lag + 1
        lax.fori_loop(p * chunks, middle, step, 0)
        paired = p - 1 < 2 * both

        @pl.when(p == 0)
        def _():
            low_first()

        @pl.when(jnp.logical_and(p >= 1, jnp.logical_and(paired, p % 2 == 0)))
        def _():
            finish(jnp.maximum(p - 2, 0))

        @pl.when(
            jnp.logical_and(p >= 1, jnp.logical_or(jnp.logical_not(paired), p % 2 == 0))
        )
        def _():
            finish(jnp.maximum(p - 1, 0))

        lax.fori_loop(middle, (p + 1) * chunks, step, 0)
        return 0

    total = (n - 1) * chunks
    lax.fori_loop(0, n - 1, phase, 0)
    lax.fori_loop(total - lag, total, lambda i, _: (cross(i), 0)[1], 0)
    low_second()
    if n % 2 == 1:

        @pl.when(2 * both == n - 1)
        def _():
            finish(jnp.int32(n - 3))

    finish(jnp.int32(n - 2))

    half = HEAD_SIZE // 2

    def rotate(v, direction):
        turned = pltpu.roll(v, half, 1) * sin_ref[...]
        return v * cos_ref[...] + (turned if direction > 0 else -turned)

    for c in range(key_cols // HEAD_SIZE):
        cols = pl.ds(c * HEAD_SIZE, HEAD_SIZE)
        raw = out_ref[:, pl.ds(query_cols + c * HEAD_SIZE, HEAD_SIZE)]
        kv[s, :, cols] = rotate(raw, 1).astype(jnp.bfloat16)
    kv[s, :, pl.ds(key_cols, key_cols)] = out_ref[
        :, pl.ds(query_cols + key_cols, key_cols)
    ].astype(jnp.bfloat16)
    kv_copy = pltpu.make_async_remote_copy(
        src_ref=kv.at[s], dst_ref=kv.at[s], send_sem=kv_sem.at[0], recv_sem=kv_sem.at[1],
        device_id={"seq": 1 - s}, device_id_type=MESH,
    )
    kv_copy.start()
    pltpu.make_async_remote_copy(
        src_ref=kv.at[1 - s], dst_ref=kv.at[1 - s], send_sem=kv_sem.at[0],
        recv_sem=kv_sem.at[1], device_id={"seq": 1 - s}, device_id_type=MESH,
    ).wait_recv()

    scale = 1.0 / math.sqrt(HEAD_SIZE)
    grouping = query_cols // key_cols

    def dot(a, b, da, db):
        return lax.dot_general(
            a, b, (((da,), (db,)), ((), ())), preferred_element_type=jnp.float32
        )

    def head(j, _):
        cols = pl.ds(pl.multiple_of(j * HEAD_SIZE, HEAD_SIZE), HEAD_SIZE)
        at = pl.multiple_of((j // grouping) * HEAD_SIZE, HEAD_SIZE)
        keys = kv[:, :, pl.ds(at, HEAD_SIZE)].reshape(2 * row_count, HEAD_SIZE)
        values = kv[:, :, pl.ds(at + key_cols, HEAD_SIZE)].reshape(2 * row_count, HEAD_SIZE)
        query = rotate(out_ref[:, cols], 1).astype(jnp.bfloat16)
        scores = dot(query, keys, 1, 1) * scale + bias[...]
        raised = jnp.exp(scores - jnp.max(scores, axis=1, keepdims=True))
        probability = raised * (1.0 / jnp.sum(raised, axis=1, keepdims=True))
        att_ref[:, cols] = dot(probability.astype(jnp.bfloat16), values, 1, 0).astype(
            jnp.bfloat16
        )
        dprob = dot(cot[:, cols], values, 1, 1)
        delta = jnp.sum(probability * dprob, axis=1, keepdims=True)
        dscore = (probability * (dprob - delta)).astype(jnp.bfloat16)
        gq[:, cols] = rotate(dot(dscore, keys, 1, 0) * scale, -1).astype(jnp.bfloat16)
        return 0

    lax.fori_loop(0, query_cols // HEAD_SIZE, head, 0, unroll=3)

    mid[0] = chosen(dot(ups[...], gq[...], 1, 1))
    for c in mid_copies:
        c.start()
    down_half = width // 2
    up_half = query_cols // 2

    def up_term(h):
        return dot(spread[...], gq[:, pl.ds(pl.multiple_of(h * up_half, 128), up_half)], 1, 0)

    def down_term(m, h):
        return dot(m, xq[:, pl.ds(pl.multiple_of(h * down_half, 128), down_half)], 1, 0)

    give[:, pl.ds(down_half, up_half)] = up_term(1 - s)
    for c in mid_copies:
        c.wait_recv()
    spread_mid = spread_out(mid)
    give[:, pl.ds(0, down_half)] = down_term(spread_mid, 1 - s)
    swap = pltpu.make_async_remote_copy(
        src_ref=give, dst_ref=got, send_sem=got_sem.at[0], recv_sem=got_sem.at[1],
        device_id={"seq": 1 - s}, device_id_type=MESH,
    )
    swap.start()
    mine_up = up_term(s)
    mine_down = down_term(spread_mid, s)
    swap.wait_recv()
    keep[:, :, pl.ds(0, down_half)] = (mine_down + got[:, pl.ds(0, down_half)]).reshape(
        n, rank, down_half
    )
    keep[:, :, pl.ds(down_half, up_half)] = (
        mine_up + got[:, pl.ds(down_half, up_half)]
    ).reshape(n, rank, up_half)
    gath_copies = [
        pltpu.make_async_remote_copy(
            src_ref=keep.at[lax.rem(z + k, n)], dst_ref=gath.at[k],
            send_sem=gath_send.at[k], recv_sem=gath_recv.at[k],
            device_id={"dp": lax.rem(z + k, n)}, device_id_type=MESH,
        )
        for k in range(1, n)
    ]
    for c in gath_copies:
        c.start()
    total_grad = keep[z]
    for k, c in enumerate(gath_copies):
        c.wait_recv()
        total_grad = total_grad + gath[k + 1]
    down_ref[...] = total_grad[:, :down_half]
    up_ref[...] = total_grad[:, down_half:]

    for k in range(1, n):
        pack_swap(k, s).wait_send()
    for c in pack_copies + low_copies + mid_copies + gath_copies + [kv_copy, swap]:
        c.wait_send()

    def drain(i, _):
        d = i // chunks
        c = i % chunks
        mine = d == z

        @pl.when(jnp.logical_and(d >= z, z > 0))
        def _():
            to_below(d, c).wait_send()

        @pl.when(jnp.logical_and(d <= z, z < n - 1))
        def _():
            to_above(d, c).wait_send()

        @pl.when(jnp.logical_not(mine))
        def _():
            to_group(d, c).wait_send()
            to_core(d, g, c, 0).wait_send()
            to_core(d, 1 - g, c, 1).wait_send()

        return 0

    lax.fori_loop(0, n * chunks, drain, 0)


def whole(
    tokens, query_weight, key_weight, value_weight, pack, cotangent, lengths, adapters, rows
):
    n = lax.axis_size("dp")
    owners = lax.axis_size("owner")
    row_count, width = tokens.shape
    depth, query_cols = query_weight.shape
    key_cols = key_weight.shape[1]
    cols = query_cols + 2 * key_cols
    rank = pack.shape[0] // 2
    wide = n * rank
    quarter = width // owners
    summed = (quarter + query_cols) // 2
    piece = depth // 4
    chunks = max(c for c in range(1, 9) if piece % c == 0 and (piece // c) % 16 == 0)
    presplit = depth % 128 != 0
    split = tokens
    if presplit:
        split = jnp.transpose(tokens.reshape(row_count, n, depth), (1, 0, 2))
    length = 2 * row_count
    angles = np.arange(length)[:, None] * rope_base ** (
        -np.arange(HEAD_SIZE // 2)[None, :] * 2.0 / HEAD_SIZE
    )
    cosines = np.concatenate([np.cos(angles), np.cos(angles)], axis=1).astype(np.float32)
    sines = np.concatenate([-np.sin(angles), np.sin(angles)], axis=1).astype(np.float32)
    dma = pltpu.SemaphoreType.DMA
    bf16 = jnp.bfloat16
    f32 = jnp.float32
    return pl.pallas_call(
        functools.partial(whole_kernel, n, owners, chunks, presplit),
        out_shape=(
            jax.ShapeDtypeStruct((row_count, query_cols), bf16),
            jax.ShapeDtypeStruct((rank, quarter // 2), f32),
            jax.ShapeDtypeStruct((rank, query_cols // 2), f32),
        ),
        in_specs=[pl.BlockSpec(memory_space=pl.ANY)] * 7
        + [pl.BlockSpec(memory_space=pltpu.SMEM)] * 3
        + [pl.BlockSpec(memory_space=pl.ANY)] * 2,
        out_specs=(pl.BlockSpec(memory_space=pltpu.VMEM),) * 3,
        scratch_shapes=[
            pltpu.VMEM((row_count, cols), f32),
            pltpu.VMEM((n, depth, cols), bf16),
            pltpu.VMEM((n, row_count, depth), bf16),
            pltpu.VMEM((row_count, quarter), bf16),
            pltpu.VMEM((n,) + pack.shape, bf16),
            pltpu.VMEM((row_count, query_cols), bf16),
            pltpu.VMEM((wide, query_cols), bf16),
            pltpu.VMEM((wide, row_count), bf16),
            pltpu.VMEM((owners, rank, row_count), f32),
            pltpu.VMEM((owners, rank, row_count), f32),
            pltpu.VMEM((2, row_count, 2 * key_cols), bf16),
            pltpu.VMEM((row_count, 2 * row_count), f32),
            pltpu.VMEM((row_count, query_cols), bf16),
            pltpu.VMEM((wide, summed), f32),
            pltpu.VMEM((wide, summed), f32),
            pltpu.VMEM((n, rank, summed), f32),
            pltpu.VMEM((n, rank, summed), f32),
            pltpu.VMEM((row_count, HEAD_SIZE), f32),
            pltpu.VMEM((row_count, HEAD_SIZE), f32),
            pltpu.VMEM((wide, row_count), f32),
            dma((8,)),
            dma((n,)),
            dma((n, chunks)),
            dma((n, chunks)),
            dma((n, chunks)),
            dma((n, chunks, 2)),
            dma((n, chunks)),
            dma((n, chunks)),
            dma((n, chunks, 2)),
            dma((n,)),
            dma((n,)),
            dma((n,)),
            dma((n,)),
            dma((owners,)),
            dma((owners,)),
            dma((owners,)),
            dma((owners,)),
            dma((2,)),
            dma((2,)),
            dma((n,)),
            dma((n,)),
        ],
        compiler_params=pltpu.CompilerParams(
            collective_id=0, has_side_effects=True, vmem_limit_bytes=56 * 2**20
        ),
        cost_estimate=pl.CostEstimate(
            flops=2 * row_count * n * depth * cols,
            bytes_accessed=2 * n * depth * cols,
            transcendentals=0,
        ),
    )(
        split, tokens, query_weight, key_weight, value_weight, pack, cotangent,
        lengths, adapters, rows, jnp.asarray(cosines), jnp.asarray(sines),
    )


def shards(
    tokens,
    document_lengths,
    document_adapter,
    adapter_stored_row,
    query_weight,
    key_weight,
    value_weight,
    adapter_down_weight,
    adapter_up_weight,
    output_cotangent,
):
    line = jnp.concatenate([adapter_up_weight[0], jnp.transpose(adapter_down_weight[0])], axis=1)
    middle = line.shape[1] // 2
    pack = jnp.concatenate([line[:, :middle], line[:, middle:]], axis=0)
    pack = jnp.pad(pack, ((0, 0), (0, -middle % 256)))
    attended, grad_down, grad_up = whole(
        tokens, query_weight, key_weight, value_weight, pack, output_cotangent,
        document_lengths, document_adapter, adapter_stored_row,
    )
    return (attended, jnp.transpose(grad_down)[None], grad_up[None])


def solution(mesh):
    in_specs = (
        P(("groups", "dp", "seq"), None),
        P(("groups", "dp"), None),
        P(("groups", "dp"), None),
        P(),
        P("dp", "owner"),
        P("dp", "owner"),
        P("dp", "owner"),
        P("dp", "owner", None),
        P("dp", None, "owner"),
        P(("groups", "dp", "seq"), "owner"),
    )
    out_specs = (
        P(("groups", "dp", "seq"), "owner"),
        P(("groups", "dp"), ("owner", "seq"), None),
        P(("groups", "dp"), None, ("owner", "seq")),
    )
    return jax.shard_map(shards, mesh=mesh, in_specs=in_specs, out_specs=out_specs, check_vma=False)
```

```python
import functools
import math

import jax
import jax.numpy as jnp
import numpy as np
from jax import lax
from jax.experimental import pallas as pl
from jax.experimental.pallas import tpu as pltpu
from jax.sharding import PartitionSpec as P

MESH = pl.DeviceIdType.MESH

HEAD_SIZE = 128


rope_base = 1000000.0
neg_big = -1e30


def whole_kernel(
    n, owners, chunks, presplit,
    x_ref, xq_ref, wq_ref, wk_ref, wv_ref, pack_ref, cot_ref,
    lengths_ref, adapters_ref, rows_ref, cos_hbm, sin_hbm,
    att_ref, down_ref, up_ref,
    out_ref, held, xs, xq, packs, cot, ups, spread, low, mid, kv, bias, gq,
    give, got, keep, gath, cos_ref, sin_ref, choose_ref,
    load_sem, x_sem,
    up_send, down_send, y_send, core_send, z_recv, y_recv, core_recv,
    pack_send, pack_recv, pack_out, pack_in, low_send, low_recv, mid_send, mid_recv,
    kv_sem, got_sem, gath_send, gath_recv,
):
    depth = wq_ref.shape[0]
    row_count = xq.shape[0]
    query_cols = wq_ref.shape[1]
    key_cols = wk_ref.shape[1]
    rank = low.shape[1]
    o = lax.axis_index("owner")
    piece = depth // 4
    rows = piece // chunks
    g = lax.axis_index("groups")
    z = lax.axis_index("dp")
    s = lax.axis_index("seq")
    above = n - 1 - z
    below = z
    both = jnp.minimum(above, below)

    copies = []
    at = 0
    for i, ref in enumerate((wq_ref, wk_ref, wv_ref)):
        width = ref.shape[1]
        copies.append(
            pltpu.make_async_copy(ref, held.at[z, :, pl.ds(at, width)], load_sem.at[i])
        )
        at += width
    x_copies = []
    for d in range(n):
        src = x_ref.at[d] if presplit else x_ref.at[:, pl.ds(d * depth, depth)]
        x_copies.append(pltpu.make_async_copy(src, xs.at[d], x_sem.at[d]))
    width = xq.shape[1]
    x_copies.append(
        pltpu.make_async_copy(
            xq_ref.at[:, pl.ds(pl.multiple_of(o * width, 128), width)], xq, load_sem.at[3]
        )
    )
    x_copies.append(pltpu.make_async_copy(cot_ref, cot, load_sem.at[4]))
    for i, (src, dst) in enumerate(((cos_hbm, cos_ref), (sin_hbm, sin_ref))):
        first = pl.multiple_of(s * row_count, 8)
        x_copies.append(
            pltpu.make_async_copy(src.at[pl.ds(first, row_count), :], dst, load_sem.at[6 + i])
        )
    copies.append(pltpu.make_async_copy(pack_ref, packs.at[z], load_sem.at[5]))
    for c in copies + x_copies:
        c.start()

    barrier = pltpu.get_barrier_semaphore()
    pl.semaphore_signal(barrier, inc=1, device_id={"groups": 1 - g}, device_id_type=MESH)
    pl.semaphore_signal(barrier, inc=1, device_id={"seq": 1 - s}, device_id_type=MESH)
    for k in range(1, n):
        pl.semaphore_signal(
            barrier, inc=1, device_id={"dp": lax.rem(z + k, n)}, device_id_type=MESH
        )
    for k in range(1, owners):
        pl.semaphore_signal(
            barrier, inc=1, device_id={"owner": lax.rem(o + k, owners)}, device_id_type=MESH
        )
    pl.semaphore_wait(barrier, n + owners)

    for c in copies:
        c.wait()

    def part(d, gg, ss, c):
        start = pl.multiple_of(((gg * 2 + ss) * chunks + c) * rows, 16)
        return held.at[d, pl.ds(start, rows), :]

    def move(d, gg, ss, c, send, recv, target):
        ref = part(d, gg, ss, c)
        return pltpu.make_async_remote_copy(
            src_ref=ref, dst_ref=ref, send_sem=send, recv_sem=recv,
            device_id=target, device_id_type=MESH,
        )

    def to_below(d, c):
        return move(d, g, s, c, down_send.at[d, c], z_recv.at[d, c], {"dp": jnp.maximum(z - 1, 0)})

    def to_above(d, c):
        return move(d, g, s, c, up_send.at[d, c], z_recv.at[d, c], {"dp": jnp.minimum(z + 1, n - 1)})

    def to_group(d, c):
        return move(d, g, s, c, y_send.at[d, c], y_recv.at[d, c], {"groups": 1 - g})

    def from_group(d, c):
        return move(d, 1 - g, s, c, y_send.at[d, c], y_recv.at[d, c], {"groups": 1 - g})

    def to_core(d, gg, c, k):
        return move(d, gg, s, c, core_send.at[d, c, k], core_recv.at[d, c, k], {"seq": 1 - s})

    def from_core(d, gg, c, k):
        return move(d, gg, 1 - s, c, core_send.at[d, c, k], core_recv.at[d, c, k], {"seq": 1 - s})

    def send_down(t):
        @pl.when(jnp.logical_and(z > 0, t < (above + 1) * chunks))
        def _():
            to_below(jnp.minimum(z + t // chunks, n - 1), t % chunks).start()

    def send_up(t):
        @pl.when(jnp.logical_and(z < n - 1, t < (below + 1) * chunks))
        def _():
            to_above(jnp.maximum(z - t // chunks, 0), t % chunks).start()

    ahead = min(2, chunks)
    for t in range(ahead):
        send_down(t)
        send_up(t)
    pack_half = packs.shape[2] // 2

    def pack_part(d, ss):
        return packs.at[d, :, pl.ds(pl.multiple_of(ss * pack_half, 128), pack_half)]

    pack_copies = [
        pltpu.make_async_remote_copy(
            src_ref=pack_part(z, s), dst_ref=pack_part(z, s),
            send_sem=pack_send.at[k], recv_sem=pack_recv.at[k],
            device_id={"dp": lax.rem(z + k, n)}, device_id_type=MESH,
        )
        for k in range(1, n)
    ]

    def pack_swap(k, ss):
        d = lax.rem(z - k + n, n)
        return pltpu.make_async_remote_copy(
            src_ref=pack_part(d, ss), dst_ref=pack_part(d, ss),
            send_sem=pack_out.at[k], recv_sem=pack_in.at[k],
            device_id={"seq": 1 - s}, device_id_type=MESH,
        )

    for c in pack_copies:
        c.start()
    for c in x_copies:
        c.wait()

    kpos = lax.broadcasted_iota(jnp.int32, bias.shape, 1)
    qpos = s * row_count + lax.broadcasted_iota(jnp.int32, bias.shape, 0)
    tpos = s * row_count + lax.broadcasted_iota(jnp.int32, choose_ref.shape, 1)
    begin = jnp.zeros(bias.shape, jnp.int32)
    stored = jnp.zeros(choose_ref.shape, jnp.int32)
    end = jnp.int32(0)
    for doc in range(lengths_ref.shape[1]):
        adapter = adapters_ref[0, doc]
        row = jnp.int32(0)
        for i in range(rows_ref.shape[0]):
            row = row + jnp.where(adapter == i, rows_ref[i], 0)
        begin = jnp.where(qpos >= end, end, begin)
        stored = jnp.where(tpos >= end, row, stored)
        end = end + lengths_ref[0, doc]
    row_of = lax.broadcasted_iota(jnp.int32, choose_ref.shape, 0) // rank
    choose_ref[...] = jnp.where(row_of == stored, 1.0, 0.0)
    allowed = jnp.logical_and(kpos <= qpos, kpos >= begin)
    bias[...] = jnp.where(allowed, 0.0, neg_big)

    def owner_copies(buf, send, recv):
        return [
            pltpu.make_async_remote_copy(
                src_ref=buf.at[0], dst_ref=buf.at[k],
                send_sem=send.at[k], recv_sem=recv.at[k],
                device_id={"owner": lax.rem(o + k, owners)}, device_id_type=MESH,
            )
            for k in range(1, owners)
        ]

    def chosen(wide):
        return jnp.sum((wide * choose_ref[...]).reshape(n, rank, row_count), axis=0)

    def spread_out(buf):
        total = buf[0]
        for k in range(1, owners):
            total = total + buf[k]
        total = total.astype(jnp.bfloat16).astype(jnp.float32)
        return (jnp.concatenate([total] * n, axis=0) * choose_ref[...]).astype(jnp.bfloat16)

    low_copies = owner_copies(low, low_send, low_recv)
    mid_copies = owner_copies(mid, mid_send, mid_recv)

    def low_first():
        for k, c in enumerate(pack_copies):
            c.wait_recv()
            pack_swap(k + 1, s).start()
        for k in range(1, n):
            pack_swap(k, 1 - s).wait_recv()
        wide = packs[:, :, : (query_cols + width) // 2].astype(jnp.float32)
        ups[...] = wide[:, :rank, :query_cols].reshape(n * rank, query_cols).astype(jnp.bfloat16)
        downs = jnp.concatenate([wide[:, :rank, query_cols:], wide[:, rank:, :]], axis=2)
        downs = downs.reshape(n * rank, width).astype(jnp.bfloat16)
        low[0] = chosen(
            lax.dot_general(
                downs, xq[...], (((1,), (1,)), ((), ())), preferred_element_type=jnp.float32
            )
        )
        for c in low_copies:
            c.start()

    def low_second():
        for c in low_copies:
            c.wait_recv()
        spread[...] = spread_out(low)

        def body(j, _):
            cols = pl.ds(pl.multiple_of(j * 256, 256), 256)
            out_ref[:, cols] += lax.dot_general(
                spread[...], ups[:, cols], (((0,), (0,)), ((), ())),
                preferred_element_type=jnp.float32,
            )
            return 0

        lax.fori_loop(0, query_cols // 256, body, 0)

    tile = 512
    tiles = out_ref.shape[1] // tile

    def multiply(d, first):
        def body(j, _):
            cols = pl.ds(pl.multiple_of(j * tile, tile), tile)
            term = jnp.dot(xs[d], held[d, :, cols], preferred_element_type=jnp.float32)
            if first:
                out_ref[:, cols] = term
            else:
                out_ref[:, cols] += term
            return 0

        lax.fori_loop(0, tiles, body, 0)

    multiply(z, True)

    def shard_of(k):
        paired = k < 2 * both
        half = k // 2
        single = jnp.where(above > below, z + 1 + (k - both), z - 1 - (k - both))
        return jnp.where(paired, jnp.where(k % 2 == 0, z + 1 + half, z - 1 - half), single)

    def event(i):
        paired = i < 2 * both * chunks
        t = i // 2
        t2 = i - both * chunks
        up = jnp.where(paired, i % 2 == 0, above > below)
        t = jnp.where(paired, t, t2)
        return jnp.where(up, z + 1 + t // chunks, z - 1 - t // chunks), t % chunks

    def land(d, c):
        to_below(d, c).wait_recv()
        to_core(d, g, c, 0).start()

    lag = min(3, chunks - 1)

    def step(t, _):
        @pl.when(t < above * chunks)
        def _():
            land(jnp.minimum(z + 1 + t // chunks, n - 1), t % chunks)

        @pl.when(t < below * chunks)
        def _():
            land(jnp.maximum(z - 1 - t // chunks, 0), t % chunks)

        send_down(t + ahead)
        send_up(t + ahead)
        to_group(*event(t)).start()

        @pl.when(t >= lag)
        def _():
            cross(t - lag)

        return 0

    def cross(i):
        d, c = event(i)
        from_group(d, c).wait_recv()
        to_core(d, 1 - g, c, 1).start()

    def finish(k):
        d = shard_of(k)

        def body(c, _):
            from_core(d, g, c, 0).wait_recv()
            from_core(d, 1 - g, c, 1).wait_recv()
            return 0

        lax.fori_loop(0, chunks, body, 0)
        multiply(d, False)

    def phase(p, _):
        middle = p * chunks + lag + 1
        lax.fori_loop(p * chunks, middle, step, 0)
        paired = p - 1 < 2 * both

        @pl.when(p == 0)
        def _():
            low_first()

        @pl.when(p == min(1, n - 2))
        def _():
            low_second()

        @pl.when(jnp.logical_and(p >= 1, jnp.logical_and(paired, p % 2 == 0)))
        def _():
            finish(jnp.maximum(p - 2, 0))

        @pl.when(
            jnp.logical_and(p >= 1, jnp.logical_or(jnp.logical_not(paired), p % 2 == 0))
        )
        def _():
            finish(jnp.maximum(p - 1, 0))

        lax.fori_loop(middle, (p + 1) * chunks, step, 0)
        return 0

    total = (n - 1) * chunks
    lax.fori_loop(0, n - 1, phase, 0)
    lax.fori_loop(total - lag, total, lambda i, _: (cross(i), 0)[1], 0)
    if n % 2 == 1:

        @pl.when(2 * both == n - 1)
        def _():
            finish(jnp.int32(n - 3))

    finish(jnp.int32(n - 2))

    half = HEAD_SIZE // 2

    def rotate(v, direction):
        turned = pltpu.roll(v, half, 1) * sin_ref[...]
        return v * cos_ref[...] + (turned if direction > 0 else -turned)

    for c in range(key_cols // HEAD_SIZE):
        cols = pl.ds(c * HEAD_SIZE, HEAD_SIZE)
        raw = out_ref[:, pl.ds(query_cols + c * HEAD_SIZE, HEAD_SIZE)]
        kv[s, :, cols] = rotate(raw, 1).astype(jnp.bfloat16)
    kv[s, :, pl.ds(key_cols, key_cols)] = out_ref[
        :, pl.ds(query_cols + key_cols, key_cols)
    ].astype(jnp.bfloat16)
    kv_copy = pltpu.make_async_remote_copy(
        src_ref=kv.at[s], dst_ref=kv.at[s], send_sem=kv_sem.at[0], recv_sem=kv_sem.at[1],
        device_id={"seq": 1 - s}, device_id_type=MESH,
    )
    kv_copy.start()
    pltpu.make_async_remote_copy(
        src_ref=kv.at[1 - s], dst_ref=kv.at[1 - s], send_sem=kv_sem.at[0],
        recv_sem=kv_sem.at[1], device_id={"seq": 1 - s}, device_id_type=MESH,
    ).wait_recv()

    scale = 1.0 / math.sqrt(HEAD_SIZE)
    grouping = query_cols // key_cols

    def dot(a, b, da, db):
        return lax.dot_general(
            a, b, (((da,), (db,)), ((), ())), preferred_element_type=jnp.float32
        )

    def head(j, _):
        cols = pl.ds(pl.multiple_of(j * HEAD_SIZE, HEAD_SIZE), HEAD_SIZE)
        at = pl.multiple_of((j // grouping) * HEAD_SIZE, HEAD_SIZE)
        keys = kv[:, :, pl.ds(at, HEAD_SIZE)].reshape(2 * row_count, HEAD_SIZE)
        values = kv[:, :, pl.ds(at + key_cols, HEAD_SIZE)].reshape(2 * row_count, HEAD_SIZE)
        query = rotate(out_ref[:, cols], 1).astype(jnp.bfloat16)
        scores = dot(query, keys, 1, 1) * scale + bias[...]
        raised = jnp.exp(scores - jnp.max(scores, axis=1, keepdims=True))
        probability = raised * (1.0 / jnp.sum(raised, axis=1, keepdims=True))
        att_ref[:, cols] = dot(probability.astype(jnp.bfloat16), values, 1, 0).astype(
            jnp.bfloat16
        )
        dprob = dot(cot[:, cols], values, 1, 1)
        delta = jnp.sum(probability * dprob, axis=1, keepdims=True)
        dscore = (probability * (dprob - delta)).astype(jnp.bfloat16)
        gq[:, cols] = rotate(dot(dscore, keys, 1, 0) * scale, -1).astype(jnp.bfloat16)
        return 0

    lax.fori_loop(0, query_cols // HEAD_SIZE, head, 0, unroll=6)

    mid[0] = chosen(dot(ups[...], gq[...], 1, 1))
    for c in mid_copies:
        c.start()
    down_half = width // 2
    up_half = query_cols // 2

    def up_term(h):
        return dot(spread[...], gq[:, pl.ds(pl.multiple_of(h * up_half, 128), up_half)], 1, 0)

    def down_term(m, h):
        return dot(m, xq[:, pl.ds(pl.multiple_of(h * down_half, 128), down_half)], 1, 0)

    give[:, pl.ds(down_half, up_half)] = up_term(1 - s)
    for c in mid_copies:
        c.wait_recv()
    spread_mid = spread_out(mid)
    give[:, pl.ds(0, down_half)] = down_term(spread_mid, 1 - s)
    swap = pltpu.make_async_remote_copy(
        src_ref=give, dst_ref=got, send_sem=got_sem.at[0], recv_sem=got_sem.at[1],
        device_id={"seq": 1 - s}, device_id_type=MESH,
    )
    swap.start()
    mine_up = up_term(s)
    mine_down = down_term(spread_mid, s)
    swap.wait_recv()
    keep[:, :, pl.ds(0, down_half)] = (mine_down + got[:, pl.ds(0, down_half)]).reshape(
        n, rank, down_half
    )
    keep[:, :, pl.ds(down_half, up_half)] = (
        mine_up + got[:, pl.ds(down_half, up_half)]
    ).reshape(n, rank, up_half)
    gath_copies = [
        pltpu.make_async_remote_copy(
            src_ref=keep.at[lax.rem(z + k, n)], dst_ref=gath.at[k],
            send_sem=gath_send.at[k], recv_sem=gath_recv.at[k],
            device_id={"dp": lax.rem(z + k, n)}, device_id_type=MESH,
        )
        for k in range(1, n)
    ]
    for c in gath_copies:
        c.start()
    total_grad = keep[z]
    for k, c in enumerate(gath_copies):
        c.wait_recv()
        total_grad = total_grad + gath[k + 1]
    down_ref[...] = total_grad[:, :down_half]
    up_ref[...] = total_grad[:, down_half:]

    for k in range(1, n):
        pack_swap(k, s).wait_send()
    for c in pack_copies + low_copies + mid_copies + gath_copies + [kv_copy, swap]:
        c.wait_send()

    def drain(i, _):
        d = i // chunks
        c = i % chunks
        mine = d == z

        @pl.when(jnp.logical_and(d >= z, z > 0))
        def _():
            to_below(d, c).wait_send()

        @pl.when(jnp.logical_and(d <= z, z < n - 1))
        def _():
            to_above(d, c).wait_send()

        @pl.when(jnp.logical_not(mine))
        def _():
            to_group(d, c).wait_send()
            to_core(d, g, c, 0).wait_send()
            to_core(d, 1 - g, c, 1).wait_send()

        return 0

    lax.fori_loop(0, n * chunks, drain, 0)


def whole(
    tokens, query_weight, key_weight, value_weight, pack, cotangent, lengths, adapters, rows
):
    n = lax.axis_size("dp")
    owners = lax.axis_size("owner")
    row_count, width = tokens.shape
    depth, query_cols = query_weight.shape
    key_cols = key_weight.shape[1]
    cols = query_cols + 2 * key_cols
    rank = pack.shape[0] // 2
    wide = n * rank
    quarter = width // owners
    summed = (quarter + query_cols) // 2
    piece = depth // 4
    chunks = max(c for c in range(1, 9) if piece % c == 0 and (piece // c) % 16 == 0)
    presplit = depth % 128 != 0
    split = tokens
    if presplit:
        split = jnp.transpose(tokens.reshape(row_count, n, depth), (1, 0, 2))
    length = 2 * row_count
    angles = np.arange(length)[:, None] * rope_base ** (
        -np.arange(HEAD_SIZE // 2)[None, :] * 2.0 / HEAD_SIZE
    )
    cosines = np.concatenate([np.cos(angles), np.cos(angles)], axis=1).astype(np.float32)
    sines = np.concatenate([-np.sin(angles), np.sin(angles)], axis=1).astype(np.float32)
    dma = pltpu.SemaphoreType.DMA
    bf16 = jnp.bfloat16
    f32 = jnp.float32
    return pl.pallas_call(
        functools.partial(whole_kernel, n, owners, chunks, presplit),
        out_shape=(
            jax.ShapeDtypeStruct((row_count, query_cols), bf16),
            jax.ShapeDtypeStruct((rank, quarter // 2), f32),
            jax.ShapeDtypeStruct((rank, query_cols // 2), f32),
        ),
        in_specs=[pl.BlockSpec(memory_space=pl.ANY)] * 7
        + [pl.BlockSpec(memory_space=pltpu.SMEM)] * 3
        + [pl.BlockSpec(memory_space=pl.ANY)] * 2,
        out_specs=(pl.BlockSpec(memory_space=pltpu.VMEM),) * 3,
        scratch_shapes=[
            pltpu.VMEM((row_count, cols), f32),
            pltpu.VMEM((n, depth, cols), bf16),
            pltpu.VMEM((n, row_count, depth), bf16),
            pltpu.VMEM((row_count, quarter), bf16),
            pltpu.VMEM((n,) + pack.shape, bf16),
            pltpu.VMEM((row_count, query_cols), bf16),
            pltpu.VMEM((wide, query_cols), bf16),
            pltpu.VMEM((wide, row_count), bf16),
            pltpu.VMEM((owners, rank, row_count), f32),
            pltpu.VMEM((owners, rank, row_count), f32),
            pltpu.VMEM((2, row_count, 2 * key_cols), bf16),
            pltpu.VMEM((row_count, 2 * row_count), f32),
            pltpu.VMEM((row_count, query_cols), bf16),
            pltpu.VMEM((wide, summed), f32),
            pltpu.VMEM((wide, summed), f32),
            pltpu.VMEM((n, rank, summed), f32),
            pltpu.VMEM((n, rank, summed), f32),
            pltpu.VMEM((row_count, HEAD_SIZE), f32),
            pltpu.VMEM((row_count, HEAD_SIZE), f32),
            pltpu.VMEM((wide, row_count), f32),
            dma((8,)),
            dma((n,)),
            dma((n, chunks)),
            dma((n, chunks)),
            dma((n, chunks)),
            dma((n, chunks, 2)),
            dma((n, chunks)),
            dma((n, chunks)),
            dma((n, chunks, 2)),
            dma((n,)),
            dma((n,)),
            dma((n,)),
            dma((n,)),
            dma((owners,)),
            dma((owners,)),
            dma((owners,)),
            dma((owners,)),
            dma((2,)),
            dma((2,)),
            dma((n,)),
            dma((n,)),
        ],
        compiler_params=pltpu.CompilerParams(
            collective_id=0, has_side_effects=True, vmem_limit_bytes=56 * 2**20
        ),
        cost_estimate=pl.CostEstimate(
            flops=2 * row_count * n * depth * cols,
            bytes_accessed=2 * n * depth * cols,
            transcendentals=0,
        ),
    )(
        split, tokens, query_weight, key_weight, value_weight, pack, cotangent,
        lengths, adapters, rows, jnp.asarray(cosines), jnp.asarray(sines),
    )


def shards(
    tokens,
    document_lengths,
    document_adapter,
    adapter_stored_row,
    query_weight,
    key_weight,
    value_weight,
    adapter_down_weight,
    adapter_up_weight,
    output_cotangent,
):
    line = jnp.concatenate([adapter_up_weight[0], jnp.transpose(adapter_down_weight[0])], axis=1)
    middle = line.shape[1] // 2
    pack = jnp.concatenate([line[:, :middle], line[:, middle:]], axis=0)
    pack = jnp.pad(pack, ((0, 0), (0, -middle % 256)))
    attended, grad_down, grad_up = whole(
        tokens, query_weight, key_weight, value_weight, pack, output_cotangent,
        document_lengths, document_adapter, adapter_stored_row,
    )
    return (attended, jnp.transpose(grad_down)[None], grad_up[None])


def solution(mesh):
    in_specs = (
        P(("groups", "dp", "seq"), None),
        P(("groups", "dp"), None),
        P(("groups", "dp"), None),
        P(),
        P("dp", "owner"),
        P("dp", "owner"),
        P("dp", "owner"),
        P("dp", "owner", None),
        P("dp", None, "owner"),
        P(("groups", "dp", "seq"), "owner"),
    )
    out_specs = (
        P(("groups", "dp", "seq"), "owner"),
        P(("groups", "dp"), ("owner", "seq"), None),
        P(("groups", "dp"), None, ("owner", "seq")),
    )
    return jax.shard_map(shards, mesh=mesh, in_specs=in_specs, out_specs=out_specs, check_vma=False)
```
